256 devices in a mesh: dp: 32 (over x, y, core), vocab: 8 (over z).
Axes of the slice: x: 4, y: 4, z: 8, core: 2. Of those that a mesh axis runs over, the one named last changes fastest.
Arguments:
- student_hidden: bfloat16 [512, 4096], P('dp'), may hold values from -18 to 18
- teacher_hidden: bfloat16 [512, 4096], P('dp'), may hold values from -18 to 18
- student_head: bfloat16 [4096, 98304], P('dp', 'vocab'), may hold values from -0.75 to 0.75
- teacher_head: bfloat16 [4096, 98304], P('vocab', 'dp'), may hold values from -0.75 to 0.75
- sampled_ids: int32 [512], P('dp'), may hold values from 0 to 98303
Outputs:
- grad_hidden: bfloat16 [512, 4096], P('dp')
- token_loss: float32 [512], P('dp')
The draws below stay inside these ranges and needn't reach their ends.
All inputs are finite; a program needn't handle non-finite values.
Results may differ from the reference program's by a relative error of at most 0.0052.
Values may be sent and summed in bfloat16 or wider, within the bound.
No kernel may reach another device: no remote copies, remote signals or barrier semaphores. Data moves between devices by JAX's collectives and lax.ppermute only.
A program may use at most 64 MiB of HBM per device.

```python
import math
import jax
import jax.numpy as jnp

D = 4096
TOKENS = 512
VOCAB = 98304


def row_scales(key, rows, low, high):
    return jnp.exp(jax.random.uniform(key, (rows, 1), jnp.float32, math.log(low), math.log(high)))


def draw_student_hidden(key, part):
    key = jax.random.fold_in(key, 11)
    scale_key, value_key = jax.random.split(key, 2)
    scales = row_scales(scale_key, TOKENS, 1.5, 15.0)
    values = jnp.clip(jax.random.normal(value_key, (TOKENS, D), jnp.float32), -6.0, 6.0)
    return (values * scales * 0.125).astype(jnp.bfloat16)


def draw_teacher_hidden(key, part):
    key = jax.random.fold_in(key, 12)
    scale_key, value_key = jax.random.split(key, 2)
    scales = row_scales(scale_key, TOKENS, 1.5, 15.0)
    values = jnp.clip(jax.random.normal(value_key, (TOKENS, D), jnp.float32), -6.0, 6.0)
    return (values * scales * 0.125).astype(jnp.bfloat16)


def place_ends(drawn, key, low, top_value):
    longest = drawn.shape.index(max(drawn.shape))
    spots = []
    for shift in (0, 1):
        where = [jax.random.randint(jax.random.fold_in(key, axis), (), 0, length) for axis, length in enumerate(drawn.shape)]
        where[longest] = (where[longest] + shift) % drawn.shape[longest]
        spots.append(tuple(where))
    return drawn.at[spots[0]].set(low).at[spots[1]].set(top_value)


def levels(rng, extent, pieces, smallest, high):
    def one(dim, parts):
        steps = jax.random.uniform(jax.random.fold_in(jax.random.fold_in(rng, 6), dim), (parts,), jnp.float32, smallest / len(pieces), high / len(pieces))
        return jnp.repeat(jnp.exp(steps), extent[dim] // parts).reshape((-1,) + (1,) * (len(extent) - dim - 1))

    loudness = one(*pieces[0])
    for cut in pieces[1:]:
        loudness = loudness * one(*cut)
    return loudness


def scatter_about(rng, dims, width, limit, cuts=(), kind=jnp.bfloat16):
    drawn = width * jax.random.normal(rng, dims, jnp.float32)
    if cuts:
        drawn = drawn * levels(rng, dims, cuts, -0.22, 0.18)
    return jnp.clip(drawn, -limit, limit).astype(kind)


def setup_inputs(seed: int = 0) -> dict:
    key_list = jax.random.split(jax.random.key(seed), 6)
    return {
        "student_hidden": draw_student_hidden(jax.random.fold_in(key_list[5], 71), 0),
        "teacher_hidden": draw_teacher_hidden(jax.random.fold_in(key_list[5], 71), 0),
        "student_head": scatter_about(key_list[2], (D, VOCAB), (D // 64) ** -0.5, 0.75, ((0, 32), (1, 8))),
        "teacher_head": scatter_about(key_list[3], (D, VOCAB), (D // 64) ** -0.5, 0.75, ((0, 8), (1, 32))),
        "sampled_ids": place_ends(jax.random.randint(key_list[4], (TOKENS,), 0, VOCAB), jax.random.fold_in(key_list[4], 1), 0, VOCAB - 1).astype(jnp.int32),
    }


ce_weight = 0.5


def normalizer(logits):
    top = jnp.max(logits, axis=1, keepdims=True)
    return top + jnp.log(jnp.sum(jnp.exp(logits - top), axis=1, keepdims=True))


def reference(student_hidden, teacher_hidden, student_head, teacher_head, sampled_ids):
    student_logits = jnp.dot(student_hidden, student_head, preferred_element_type=jnp.float32)
    teacher_logits = jnp.dot(teacher_hidden, teacher_head, preferred_element_type=jnp.float32)
    student_norm = normalizer(student_logits)
    teacher_norm = normalizer(teacher_logits)
    student_logprob = student_logits - student_norm
    teacher_logprob = teacher_logits - teacher_norm
    student_prob = jnp.exp(student_logprob)
    divergence = jnp.sum(student_prob * (student_logits - teacher_logits), axis=1, keepdims=True) - student_norm + teacher_norm
    columns = jnp.arange(VOCAB, dtype=jnp.int32)
    hit_mask = (columns[None, :] == sampled_ids[:, None]).astype(jnp.float32)
    logit_grad = (student_prob * (student_logprob - teacher_logprob - divergence) + ce_weight * (student_prob - hit_mask)).astype(jnp.bfloat16)
    grad_hidden = jnp.dot(logit_grad, student_head.T, preferred_element_type=jnp.float32).astype(jnp.bfloat16)
    picked = jnp.take_along_axis(student_logits, sampled_ids[:, None].astype(jnp.int32), axis=1)
    token_loss = (divergence + ce_weight * (student_norm - picked))[:, 0]
    return (grad_hidden, token_loss)
```

```python
import jax
import jax.numpy as jnp
from jax import lax
from jax.sharding import Mesh, PartitionSpec as P

ce_weight = 0.5
digit = 64
lanes = 128
XYH = ("x", "yh")
XY = ("x", "yh", "yl")
DP = ("x", "yh", "yl", "c")


def swap_cores(value):
    return lax.ppermute(value, "c", [(0, 1), (1, 0)])


def in_core_order(mine, other, axis):
    first = lax.axis_index("c") == 0
    return jnp.concatenate(
        [jnp.where(first, mine, other), jnp.where(first, other, mine)], axis=axis
    )


def spread(value, axes):
    count = lax.axis_size(axes)
    copies = jnp.broadcast_to(value[None], (count,) + value.shape)
    return lax.all_to_all(copies, axes, 0, 0, tiled=True)


def merge(stats):
    student_tops, teacher_tops = stats[:, 0], stats[:, 1]
    student_top = jnp.max(student_tops, axis=0)
    teacher_top = jnp.max(teacher_tops, axis=0)
    student_scale = jnp.exp(student_tops - student_top)
    teacher_scale = jnp.exp(teacher_tops - teacher_top)
    return jnp.stack(
        [
            student_top,
            teacher_top,
            jnp.sum(stats[:, 2] * student_scale, axis=0),
            jnp.sum(stats[:, 3] * teacher_scale, axis=0),
            jnp.sum(stats[:, 4] * student_scale, axis=0),
            jnp.sum(stats[:, 5], axis=0),
        ]
    )


def local(student_hidden, teacher_hidden, student_head, teacher_head, sampled_ids):
    core = lax.axis_index("c")
    tok, width = student_hidden.shape
    xy_count = lax.axis_size(XY)
    z_count = lax.axis_size("z")
    row_part = student_head.shape[0]
    unit = teacher_head.shape[1] // z_count
    teacher_rows = teacher_head.shape[0]
    half = width // 2

    teacher_parts = teacher_head.reshape(teacher_rows, z_count, unit).transpose(1, 0, 2)
    teacher_cols = lax.all_to_all(teacher_parts, XYH, 0, 0, tiled=True)

    by_core = student_hidden.reshape(tok, xy_count, 2, row_part)
    even = by_core[:, :, 0].reshape(tok, half)
    odd = by_core[:, :, 1].reshape(tok, half)
    keep = jnp.where(core == 0, even, odd)
    give = jnp.where(core == 0, odd, even)
    teacher_slice = lax.dynamic_slice_in_dim(
        teacher_hidden, lax.axis_index("z") * teacher_rows, teacher_rows, 1
    )
    digits = jnp.stack(
        [sampled_ids // (digit * digit), sampled_ids // digit % digit, sampled_ids % digit], axis=1
    ).astype(jnp.bfloat16)
    digits = jnp.pad(digits, ((0, 0), (0, lanes - 3)))
    shared = jnp.concatenate([teacher_slice, digits], axis=1)
    received = swap_cores(jnp.concatenate([give, shared], axis=1))
    pair = in_core_order(jnp.concatenate([keep, shared], axis=1), received, 0)
    rows = lax.all_gather(pair, XY, axis=0, tiled=True)
    student_rows = rows[:, :half]
    teacher_rows_all = rows[:, half : half + teacher_rows]
    id_digits = rows[:, half + teacher_rows : half + teacher_rows + 3].astype(jnp.int32)
    all_ids = (id_digits[:, 0] * digit + id_digits[:, 1]) * digit + id_digits[:, 2]
    tokens = rows.shape[0]

    teacher_part = jnp.stack(
        [
            jnp.dot(teacher_rows_all, teacher_cols[s], preferred_element_type=jnp.float32)
            for s in range(z_count)
        ]
    )
    student_head, teacher_part = lax.optimization_barrier((student_head, teacher_part))
    teacher_logits = lax.psum_scatter(teacher_part, "z", scatter_dimension=0, tiled=False)

    parts = student_head.reshape(row_part, 2, 2, z_count, unit).transpose(3, 1, 0, 2, 4)
    parts = parts.reshape(xy_count, row_part, 2 * unit)
    student_cols = lax.all_to_all(parts, XY, 0, 0, tiled=True).reshape(half, 2 * unit)
    student_part = jnp.dot(student_rows, student_cols, preferred_element_type=jnp.float32)
    left, right = student_part[:, :unit], student_part[:, unit:]
    student_logits = jnp.where(core == 0, left, right) + swap_cores(
        jnp.where(core == 0, right, left)
    )

    xyh = lax.axis_index("x") * 2 + lax.axis_index("yh")
    owner = (lax.axis_index("z") * 2 + lax.axis_index("yl")) * 2 + core
    first_col = (owner * z_count + xyh) * unit
    column_ids = first_col + jnp.arange(unit, dtype=jnp.int32)
    hit_mask = (column_ids[None, :] == all_ids[:, None]).astype(jnp.float32)

    logit_gap = student_logits - teacher_logits
    student_top = jnp.max(student_logits, axis=1)
    teacher_top = jnp.max(teacher_logits, axis=1)
    student_exp = jnp.exp(student_logits - student_top[:, None])
    teacher_exp = jnp.exp(teacher_logits - teacher_top[:, None])
    stats = jnp.stack(
        [
            student_top,
            teacher_top,
            jnp.sum(student_exp, axis=1),
            jnp.sum(teacher_exp, axis=1),
            jnp.sum(student_exp * logit_gap, axis=1),
            jnp.sum(hit_mask * student_logits, axis=1),
        ]
    )
    stats = merge(jnp.stack([stats, swap_cores(stats)]))
    stats = merge(spread(stats, XY))
    stats = merge(spread(stats, "z"))
    student_norm = stats[0] + jnp.log(stats[2])
    teacher_norm = stats[1] + jnp.log(stats[3])
    expected_gap = stats[4] / stats[2]
    divergence = expected_gap - student_norm + teacher_norm
    every_loss = divergence + ce_weight * (student_norm - stats[5])
    own_start = lax.axis_index(DP) * tok
    token_loss = lax.dynamic_slice_in_dim(every_loss, own_start, tok, 0)

    student_prob = jnp.exp(student_logits - student_norm[:, None])
    logit_grad = (
        student_prob * (logit_gap - expected_gap[:, None])
        + ce_weight * (student_prob - hit_mask)
    ).astype(jnp.bfloat16)
    pair_grad = in_core_order(logit_grad, swap_cores(logit_grad), 1)
    grad_part = lax.dot_general(
        pair_grad, student_cols, (((1,), (1,)), ((), ())), preferred_element_type=jnp.float32
    ).astype(jnp.bfloat16)
    grad_part = grad_part.reshape(xy_count, tokens // xy_count, half)
    plane_sum = jnp.sum(
        lax.all_to_all(grad_part, XY, 0, 0, tiled=True).astype(jnp.float32), axis=0
    )
    plane_part = plane_sum.astype(jnp.bfloat16).reshape(z_count, -1, half)
    total = jnp.sum(
        lax.all_to_all(plane_part, "z", 0, 0, tiled=True).astype(jnp.float32), axis=0
    ).astype(jnp.bfloat16)
    grads = spread(total, "z").reshape(2, tok, half)
    mine = jnp.where(core == 0, grads[0], grads[1])
    other = swap_cores(jnp.where(core == 0, grads[1], grads[0]))
    grad_hidden = in_core_order(
        mine.reshape(tok, xy_count, 1, row_part), other.reshape(tok, xy_count, 1, row_part), 2
    ).reshape(tok, width)
    return (grad_hidden, token_loss)


def solution(mesh):
    fine = Mesh(mesh.devices.reshape(4, 2, 2, 2, 8), ("x", "yh", "yl", "c", "z"))
    in_specs = (P(DP, None), P(DP, None), P(DP, "z"), P("z", DP), P(DP))
    out_specs = (P(DP, None), P(DP))
    return jax.shard_map(local, mesh=fine, in_specs=in_specs, out_specs=out_specs, check_vma=False)
```

```python
import jax
import jax.numpy as jnp
from jax import lax
from jax.experimental import pallas as pl
from jax.experimental.pallas import tpu as pltpu
from jax.sharding import Mesh, PartitionSpec as P

ce_weight = 0.5
digit = 64
lanes = 128
XYH = ("x", "yh")
XY = ("x", "yh", "yl")
DP = ("x", "yh", "yl", "c")


def swap_cores(value):
    return lax.ppermute(value, "c", [(0, 1), (1, 0)])


def in_core_order(mine, other, axis):
    first = lax.axis_index("c") == 0
    return jnp.concatenate(
        [jnp.where(first, mine, other), jnp.where(first, other, mine)], axis=axis
    )


def exchange(value, axes):
    return lax.all_to_all(value, axes, 0, 0, tiled=True)


def spread(value, axes):
    count = lax.axis_size(axes)
    return exchange(jnp.broadcast_to(value[None], (count,) + value.shape), axes)


def merge(stats):
    student_tops, teacher_tops = stats[:, 0], stats[:, 1]
    student_top = jnp.max(student_tops, axis=0)
    teacher_top = jnp.max(teacher_tops, axis=0)
    student_scale = jnp.exp(student_tops - student_top)
    teacher_scale = jnp.exp(teacher_tops - teacher_top)
    return jnp.stack(
        [
            student_top,
            teacher_top,
            jnp.sum(stats[:, 2] * student_scale, axis=0),
            jnp.sum(stats[:, 3] * teacher_scale, axis=0),
            jnp.sum(stats[:, 4] * student_scale, axis=0),
            jnp.sum(stats[:, 5], axis=0),
        ]
    )


def teacher_kernel(rows_ref, cols_ref, out_ref):
    part = jnp.dot(rows_ref[...], cols_ref[...], preferred_element_type=jnp.float32)
    out_ref[:, 0] = part.reshape(out_ref.shape[0], out_ref.shape[2], out_ref.shape[3])


def teacher_partial(rows, head, planes, unit):
    depth, width = head.shape
    tokens = rows.shape[0]
    units = width // unit
    return pl.pallas_call(
        teacher_kernel,
        grid=(units,),
        in_specs=[
            pl.BlockSpec((tokens, depth), lambda j: (0, 0)),
            pl.BlockSpec((depth, unit), lambda j: (0, j)),
        ],
        out_specs=pl.BlockSpec((planes, 1, tokens // planes, unit), lambda j: (0, j, 0, 0)),
        out_shape=jax.ShapeDtypeStruct((planes, units, tokens // planes, unit), jnp.float32),
        compiler_params=pltpu.CompilerParams(vmem_limit_bytes=32 * 2**20),
    )(rows, head)


def regroup_kernel(head_ref, out_ref):
    unit = out_ref.shape[4]
    for j in range(out_ref.shape[0]):
        out_ref[j, 0, 0] = head_ref[:, j * unit : (j + 1) * unit]


def regroup(head, units, unit):
    rows, width = head.shape
    return pl.pallas_call(
        regroup_kernel,
        grid=(2, 2),
        in_specs=[pl.BlockSpec((rows, width // 4), lambda yl, core: (0, yl * 2 + core))],
        out_specs=pl.BlockSpec(
            (units, 1, 1, rows, unit), lambda yl, core: (0, yl, core, 0, 0)
        ),
        out_shape=jax.ShapeDtypeStruct((units, 2, 2, rows, unit), head.dtype),
        compiler_params=pltpu.CompilerParams(vmem_limit_bytes=32 * 2**20),
    )(head)


def student_kernel(core_ref, rows_ref, own_ref, pair_ref, mine_ref, other_ref):
    depth, unit = rows_ref.shape[1], mine_ref.shape[1]
    for cols_ref, out_ref in ((own_ref, mine_ref), (pair_ref, other_ref)):
        cols = cols_ref[:, 0].reshape(depth, unit)
        out_ref[...] = jnp.dot(rows_ref[...], cols, preferred_element_type=jnp.float32)


def student_partial(core, rows, cols):
    tokens, depth = rows.shape
    groups, _, part, unit = cols.shape
    block = 128
    half = jax.ShapeDtypeStruct((tokens, unit), jnp.float32)
    return pl.pallas_call(
        student_kernel,
        grid_spec=pltpu.PrefetchScalarGridSpec(
            num_scalar_prefetch=1,
            grid=(tokens // block,),
            in_specs=[
                pl.BlockSpec((block, depth), lambda i, core: (i, 0)),
                pl.BlockSpec((groups, 1, part, unit), lambda i, core: (0, core[0], 0, 0)),
                pl.BlockSpec((groups, 1, part, unit), lambda i, core: (0, 1 - core[0], 0, 0)),
            ],
            out_specs=[pl.BlockSpec((block, unit), lambda i, core: (i, 0))] * 2,
        ),
        out_shape=[half, half],
        compiler_params=pltpu.CompilerParams(vmem_limit_bytes=32 * 2**20),
    )(core, rows, cols, cols)


def grad_kernel(core_ref, own_grad_ref, pair_grad_ref, own_ref, pair_ref, out_ref):
    total = None
    for grad_ref, cols_ref in ((own_grad_ref, own_ref), (pair_grad_ref, pair_ref)):
        cols = cols_ref[:, 0].reshape(out_ref.shape[1], grad_ref.shape[1])
        term = lax.dot_general(
            grad_ref[...], cols, (((1,), (1,)), ((), ())), preferred_element_type=jnp.float32
        )
        total = term if total is None else total + term
    out_ref[...] = total.astype(out_ref.dtype)


def grad_partial(core, own_grad, pair_grad, cols):
    tokens, unit = own_grad.shape
    groups, _, part, _ = cols.shape
    block = 4
    return pl.pallas_call(
        grad_kernel,
        grid_spec=pltpu.PrefetchScalarGridSpec(
            num_scalar_prefetch=1,
            grid=(groups // block,),
            in_specs=[
                pl.BlockSpec((tokens, unit), lambda i, core: (0, 0)),
                pl.BlockSpec((tokens, unit), lambda i, core: (0, 0)),
                pl.BlockSpec((block, 1, part, unit), lambda i, core: (i, core[0], 0, 0)),
                pl.BlockSpec((block, 1, part, unit), lambda i, core: (i, 1 - core[0], 0, 0)),
            ],
            out_specs=pl.BlockSpec((tokens, block * part), lambda i, core: (0, i)),
        ),
        out_shape=jax.ShapeDtypeStruct((tokens, groups * part), jnp.bfloat16),
        compiler_params=pltpu.CompilerParams(vmem_limit_bytes=32 * 2**20),
    )(core, own_grad, pair_grad, cols, cols)


def local(student_hidden, teacher_hidden, student_head, teacher_head, sampled_ids):
    core = lax.axis_index("c")
    core_id = core.reshape(1).astype(jnp.int32)
    plane = lax.axis_index("z")
    tok, width = student_hidden.shape
    xy_count = lax.axis_size(XY)
    z_count = lax.axis_size("z")
    row_part = student_head.shape[0]
    unit = teacher_head.shape[1] // z_count
    depth = teacher_head.shape[0]
    half = width // 2

    teacher_slice = lax.dynamic_slice_in_dim(teacher_hidden, plane * depth, depth, 1)
    digits = jnp.stack(
        [sampled_ids // (digit * digit), sampled_ids // digit % digit, sampled_ids % digit], axis=1
    ).astype(jnp.bfloat16)
    digits = jnp.pad(digits, ((0, 0), (0, lanes - 3)))
    shared = jnp.concatenate([teacher_slice, digits], axis=1)
    shared = in_core_order(shared, swap_cores(shared), 0)
    shared = spread(shared, XY).reshape(-1, depth + lanes)
    tokens = shared.shape[0]
    some = tokens // z_count

    teacher_part = teacher_partial(shared, teacher_head, z_count, unit)

    parts = regroup(student_head, z_count, unit).reshape(xy_count, 2, row_part, unit)
    by_core = student_hidden.reshape(tok, xy_count, 2, row_part)
    even = by_core[:, :, 0].reshape(tok, half)
    odd = by_core[:, :, 1].reshape(tok, half)
    received = swap_cores(jnp.where(core == 0, odd, even))
    student_pair = in_core_order(jnp.where(core == 0, even, odd), received, 0)

    parts, student_pair, teacher_part = lax.optimization_barrier(
        (parts, student_pair, teacher_part)
    )
    teacher_own = lax.psum_scatter(teacher_part, "z", scatter_dimension=0, tiled=False)

    student_cols = exchange(parts, XY)
    student_rows = spread(student_pair, XY).reshape(tokens, half)
    teacher_own, _ = lax.optimization_barrier((teacher_own, (student_rows, student_cols)))
    teacher_logits = exchange(teacher_own, XYH)

    mine, other = student_partial(core_id, student_rows, student_cols)
    student_logits = exchange((mine + swap_cores(other)).reshape(z_count, some, unit), "z")

    xyh = lax.axis_index("x") * 2 + lax.axis_index("yh")
    planes = jnp.arange(z_count, dtype=jnp.int32)
    owner = (planes * 2 + lax.axis_index("yl")) * 2 + core
    column_ids = ((owner * z_count + xyh) * unit)[:, None] + jnp.arange(unit, dtype=jnp.int32)
    id_digits = lax.dynamic_slice_in_dim(shared, plane * some, some, 0)[:, depth : depth + 3]
    id_digits = id_digits.astype(jnp.int32)
    ids = (id_digits[:, 0] * digit + id_digits[:, 1]) * digit + id_digits[:, 2]
    hit_mask = (column_ids[:, None, :] == ids[None, :, None]).astype(jnp.float32)

    logit_gap = student_logits - teacher_logits
    student_top = jnp.max(student_logits, axis=(0, 2))
    teacher_top = jnp.max(teacher_logits, axis=(0, 2))
    student_exp = jnp.exp(student_logits - student_top[:, None])
    teacher_exp = jnp.exp(teacher_logits - teacher_top[:, None])
    stats = jnp.stack(
        [
            student_top,
            teacher_top,
            jnp.sum(student_exp, axis=(0, 2)),
            jnp.sum(teacher_exp, axis=(0, 2)),
            jnp.sum(student_exp * logit_gap, axis=(0, 2)),
            jnp.sum(hit_mask * student_logits, axis=(0, 2)),
        ]
    )
    stats = merge(jnp.stack([stats, swap_cores(stats)]))
    stats = merge(spread(stats, XY))
    student_norm = stats[0] + jnp.log(stats[2])
    teacher_norm = stats[1] + jnp.log(stats[3])
    expected_gap = stats[4] / stats[2]
    divergence = expected_gap - student_norm + teacher_norm
    losses = divergence + ce_weight * (student_norm - stats[5])

    student_prob = jnp.exp(student_logits - student_norm[:, None])
    logit_grad = (
        student_prob * (logit_gap - expected_gap[:, None])
        + ce_weight * (student_prob - hit_mask)
    ).astype(jnp.bfloat16)
    logit_grad = exchange(logit_grad, "z").reshape(tokens, unit)
    grad_part = grad_partial(core_id, logit_grad, swap_cores(logit_grad), student_cols)
    grad_part = grad_part.reshape(xy_count, 2 * tok, half)
    plane_sum = jnp.sum(exchange(grad_part, XY).astype(jnp.float32), axis=0)
    plane_part = plane_sum.astype(jnp.bfloat16).reshape(z_count, -1, half)
    total = jnp.sum(exchange(plane_part, "z").astype(jnp.float32), axis=0).astype(jnp.bfloat16)

    high = losses.astype(jnp.bfloat16)
    rest = losses - high.astype(jnp.float32)
    middle = rest.astype(jnp.bfloat16)
    low = (rest - middle.astype(jnp.float32)).astype(jnp.bfloat16)
    terms = jnp.pad(
        jnp.stack([high, middle, low]), ((0, total.shape[0] - 3), (0, lanes - some))
    )
    final = spread(jnp.concatenate([total, terms], axis=1), "z")
    term = final[:, :3, half : half + some].astype(jnp.float32)
    every_loss = ((term[:, 2] + term[:, 1]) + term[:, 0]).reshape(tokens)
    token_loss = lax.dynamic_slice_in_dim(every_loss, lax.axis_index(DP) * tok, tok, 0)
    grads = final[:, :, :half].reshape(2, tok, half)
    mine = jnp.where(core == 0, grads[0], grads[1])
    other = swap_cores(jnp.where(core == 0, grads[1], grads[0]))
    grad_hidden = in_core_order(
        mine.reshape(tok, xy_count, 1, row_part), other.reshape(tok, xy_count, 1, row_part), 2
    ).reshape(tok, width)
    return (grad_hidden, token_loss)


def solution(mesh):
    fine = Mesh(mesh.devices.reshape(4, 2, 2, 2, 8), ("x", "yh", "yl", "c", "z"))
    in_specs = (P(DP, None), P(DP, None), P(DP, "z"), P("z", DP), P(DP))
    out_specs = (P(DP, None), P(DP))
    return jax.shard_map(local, mesh=fine, in_specs=in_specs, out_specs=out_specs, check_vma=False)
```

```python
import jax
import jax.numpy as jnp
from jax import lax
from jax.experimental import pallas as pl
from jax.experimental.pallas import tpu as pltpu
from jax.sharding import Mesh, PartitionSpec as P

ce_weight = 0.5
digit = 64
lanes = 128
big_vmem = 56 * 2**20
early_groups = 4
XYH = ("x", "yh")
XY = ("x", "yh", "yl")
DP = ("x", "yh", "yl", "c")


def swap_cores(value):
    return lax.ppermute(value, "c", [(0, 1), (1, 0)])


def in_core_order(mine, other, axis):
    first = lax.axis_index("c") == 0
    return jnp.concatenate(
        [jnp.where(first, mine, other), jnp.where(first, other, mine)], axis=axis
    )


def exchange(value, axes):
    return lax.all_to_all(value, axes, 0, 0, tiled=True)


def spread(value, axes):
    count = lax.axis_size(axes)
    return exchange(jnp.broadcast_to(value[None], (count,) + value.shape), axes)


def merge(stats):
    student_tops, teacher_tops = stats[:, 0], stats[:, 1]
    student_top = jnp.max(student_tops, axis=0)
    teacher_top = jnp.max(teacher_tops, axis=0)
    student_scale = jnp.exp(student_tops - student_top)
    teacher_scale = jnp.exp(teacher_tops - teacher_top)
    return jnp.stack(
        [
            student_top,
            teacher_top,
            jnp.sum(stats[:, 2] * student_scale, axis=0),
            jnp.sum(stats[:, 3] * teacher_scale, axis=0),
            jnp.sum(stats[:, 4] * student_scale, axis=0),
            jnp.sum(stats[:, 5], axis=0),
        ]
    )


def teacher_regroup_kernel(head_ref, out_ref):
    out_ref[0] = head_ref[...]


def teacher_regroup(head, unit):
    depth, width = head.shape
    units = width // unit
    return pl.pallas_call(
        teacher_regroup_kernel,
        grid=(units,),
        in_specs=[pl.BlockSpec((depth, unit), lambda j: (0, j))],
        out_specs=pl.BlockSpec((1, depth, unit), lambda j: (j, 0, 0)),
        out_shape=jax.ShapeDtypeStruct((units, depth, unit), head.dtype),
        compiler_params=pltpu.CompilerParams(vmem_limit_bytes=big_vmem),
    )(head)


def teacher_kernel(rows_ref, cols_ref, out_ref):
    out_ref[0] = jnp.dot(rows_ref[...], cols_ref[0], preferred_element_type=jnp.float32)


def teacher_partial(rows, cols):
    units, depth, unit = cols.shape
    tokens = rows.shape[0]
    return pl.pallas_call(
        teacher_kernel,
        grid=(units,),
        in_specs=[
            pl.BlockSpec((tokens, depth), lambda j: (0, 0)),
            pl.BlockSpec((1, depth, unit), lambda j: (j, 0, 0)),
        ],
        out_specs=pl.BlockSpec((1, tokens, unit), lambda j: (j, 0, 0)),
        out_shape=jax.ShapeDtypeStruct((units, tokens, unit), jnp.float32),
        compiler_params=pltpu.CompilerParams(vmem_limit_bytes=big_vmem),
    )(rows, cols)


def regroup_kernel(head_ref, out_ref):
    unit = out_ref.shape[4]
    for j in range(out_ref.shape[0]):
        out_ref[j, 0, 0] = head_ref[:, j * unit : (j + 1) * unit]


def regroup(head, units, unit):
    rows, width = head.shape
    return pl.pallas_call(
        regroup_kernel,
        grid=(2, 2),
        in_specs=[pl.BlockSpec((rows, width // 4), lambda yl, core: (0, yl * 2 + core))],
        out_specs=pl.BlockSpec(
            (units, 1, 1, rows, unit), lambda yl, core: (0, yl, core, 0, 0)
        ),
        out_shape=jax.ShapeDtypeStruct((units, 2, 2, rows, unit), head.dtype),
        compiler_params=pltpu.CompilerParams(vmem_limit_bytes=32 * 2**20),
    )(head)


def student_kernel(core_ref, early_ref, late_ref, own_ref, pair_ref, mine_ref, other_ref):
    unit = mine_ref.shape[1]
    split = early_groups
    for cols_ref, out_ref in ((own_ref, mine_ref), (pair_ref, other_ref)):
        first = cols_ref[:split, 0].reshape(-1, unit)
        second = cols_ref[split:, 0].reshape(-1, unit)
        out_ref[...] = jnp.dot(
            early_ref[...], first, preferred_element_type=jnp.float32
        ) + jnp.dot(late_ref[...], second, preferred_element_type=jnp.float32)


def student_partial(core, early, late, cols):
    tokens = early.shape[0]
    groups, _, part, unit = cols.shape
    block = 128
    first = early_groups * part
    half = jax.ShapeDtypeStruct((tokens, unit), jnp.float32)
    return pl.pallas_call(
        student_kernel,
        grid_spec=pltpu.PrefetchScalarGridSpec(
            num_scalar_prefetch=1,
            grid=(tokens // block,),
            in_specs=[
                pl.BlockSpec((block, first), lambda i, core: (i, 0)),
                pl.BlockSpec((block, groups * part - first), lambda i, core: (i, 0)),
                pl.BlockSpec((groups, 1, part, unit), lambda i, core: (0, core[0], 0, 0)),
                pl.BlockSpec((groups, 1, part, unit), lambda i, core: (0, 1 - core[0], 0, 0)),
            ],
            out_specs=[pl.BlockSpec((block, unit), lambda i, core: (i, 0))] * 2,
        ),
        out_shape=[half, half],
        compiler_params=pltpu.CompilerParams(vmem_limit_bytes=32 * 2**20),
    )(core, early, late, cols, cols)


def grad_kernel(core_ref, own_grad_ref, pair_grad_ref, own_ref, pair_ref, out_ref):
    total = None
    for grad_ref, cols_ref in ((own_grad_ref, own_ref), (pair_grad_ref, pair_ref)):
        cols = cols_ref[:, 0].reshape(out_ref.shape[1], grad_ref.shape[1])
        term = lax.dot_general(
            grad_ref[...], cols, (((1,), (1,)), ((), ())), preferred_element_type=jnp.float32
        )
        total = term if total is None else total + term
    out_ref[...] = total.astype(out_ref.dtype)


def grad_partial(core, own_grad, pair_grad, cols):
    tokens, unit = own_grad.shape
    groups, _, part, _ = cols.shape
    block = 4
    return pl.pallas_call(
        grad_kernel,
        grid_spec=pltpu.PrefetchScalarGridSpec(
            num_scalar_prefetch=1,
            grid=(groups // block,),
            in_specs=[
                pl.BlockSpec((tokens, unit), lambda i, core: (0, 0)),
                pl.BlockSpec((tokens, unit), lambda i, core: (0, 0)),
                pl.BlockSpec((block, 1, part, unit), lambda i, core: (i, core[0], 0, 0)),
                pl.BlockSpec((block, 1, part, unit), lambda i, core: (i, 1 - core[0], 0, 0)),
            ],
            out_specs=pl.BlockSpec((tokens, block * part), lambda i, core: (0, i)),
        ),
        out_shape=jax.ShapeDtypeStruct((tokens, groups * part), jnp.bfloat16),
        compiler_params=pltpu.CompilerParams(vmem_limit_bytes=32 * 2**20),
    )(core, own_grad, pair_grad, cols, cols)


def local(student_hidden, teacher_hidden, student_head, teacher_head, sampled_ids):
    core = lax.axis_index("c")
    core_id = core.reshape(1).astype(jnp.int32)
    plane = lax.axis_index("z")
    tok, width = student_hidden.shape
    xy_count = lax.axis_size(XY)
    z_count = lax.axis_size("z")
    row_part = student_head.shape[0]
    unit = teacher_head.shape[1] // z_count
    depth = teacher_head.shape[0]
    half = width // 2

    by_core = student_hidden.reshape(tok, xy_count, 2, row_part)
    even = by_core[:, :, 0].reshape(tok, half)
    odd = by_core[:, :, 1].reshape(tok, half)
    keep = jnp.where(core == 0, even, odd)
    give = jnp.where(core == 0, odd, even)
    teacher_slice = lax.dynamic_slice_in_dim(teacher_hidden, plane * depth, depth, 1)
    digits = jnp.stack(
        [sampled_ids // (digit * digit), sampled_ids // digit % digit, sampled_ids % digit], axis=1
    ).astype(jnp.bfloat16)
    digits = jnp.pad(digits, ((0, 0), (0, lanes - 3)))
    shared = jnp.concatenate([teacher_slice, digits], axis=1)
    received = swap_cores(jnp.concatenate([shared, give], axis=1))
    pair = in_core_order(jnp.concatenate([shared, keep], axis=1), received, 0)
    early = early_groups * row_part
    cut = depth + lanes + early
    gathered = lax.all_gather(pair[:, :cut], XY, axis=0, tiled=True)
    late_pair = pair[:, cut:]
    tokens = gathered.shape[0]
    early_rows = gathered[:, depth + lanes :]
    id_digits = gathered[:, depth : depth + 3].astype(jnp.int32)
    all_ids = (id_digits[:, 0] * digit + id_digits[:, 1]) * digit + id_digits[:, 2]

    teacher_cols = exchange(teacher_regroup(teacher_head, unit), XYH)
    teacher_part = teacher_partial(gathered[:, :depth], teacher_cols)
    student_head, late_pair, teacher_part = lax.optimization_barrier(
        (student_head, late_pair, teacher_part)
    )
    teacher_logits = lax.psum_scatter(teacher_part, "z", scatter_dimension=0, tiled=False)

    parts = regroup(student_head, z_count, unit).reshape(xy_count, 2, row_part, unit)
    student_cols = exchange(parts, XY)
    late_rows = spread(late_pair, XY).reshape(tokens, half - early)
    mine, other = student_partial(core_id, early_rows, late_rows, student_cols)
    student_logits = mine + swap_cores(other)

    xyh = lax.axis_index("x") * 2 + lax.axis_index("yh")
    owner = (plane * 2 + lax.axis_index("yl")) * 2 + core
    column_ids = (owner * z_count + xyh) * unit + jnp.arange(unit, dtype=jnp.int32)
    hit_mask = (column_ids[None, :] == all_ids[:, None]).astype(jnp.float32)

    logit_gap = student_logits - teacher_logits
    student_top = jnp.max(student_logits, axis=1)
    teacher_top = jnp.max(teacher_logits, axis=1)
    student_exp = jnp.exp(student_logits - student_top[:, None])
    teacher_exp = jnp.exp(teacher_logits - teacher_top[:, None])
    stats = jnp.stack(
        [
            student_top,
            teacher_top,
            jnp.sum(student_exp, axis=1),
            jnp.sum(teacher_exp, axis=1),
            jnp.sum(student_exp * logit_gap, axis=1),
            jnp.sum(hit_mask * student_logits, axis=1),
        ]
    )
    stats = merge(jnp.stack([stats, swap_cores(stats)]))
    stats = merge(spread(stats, XY))
    stats = merge(spread(stats, "z"))
    student_norm = stats[0] + jnp.log(stats[2])
    teacher_norm = stats[1] + jnp.log(stats[3])
    expected_gap = stats[4] / stats[2]
    divergence = expected_gap - student_norm + teacher_norm
    every_loss = divergence + ce_weight * (student_norm - stats[5])
    token_loss = lax.dynamic_slice_in_dim(every_loss, lax.axis_index(DP) * tok, tok, 0)

    student_prob = jnp.exp(student_logits - student_norm[:, None])
    logit_grad = (
        student_prob * (logit_gap - expected_gap[:, None])
        + ce_weight * (student_prob - hit_mask)
    ).astype(jnp.bfloat16)
    grad_part = grad_partial(core_id, logit_grad, swap_cores(logit_grad), student_cols)
    grad_part = grad_part.reshape(xy_count, 2 * tok, half)
    plane_sum = jnp.sum(exchange(grad_part, XY).astype(jnp.float32), axis=0)
    plane_part = plane_sum.astype(jnp.bfloat16).reshape(z_count, -1, half)
    total = jnp.sum(exchange(plane_part, "z").astype(jnp.float32), axis=0).astype(jnp.bfloat16)

    grads = spread(total, "z").reshape(2, tok, half)
    mine = jnp.where(core == 0, grads[0], grads[1])
    other = swap_cores(jnp.where(core == 0, grads[1], grads[0]))
    grad_hidden = in_core_order(
        mine.reshape(tok, xy_count, 1, row_part), other.reshape(tok, xy_count, 1, row_part), 2
    ).reshape(tok, width)
    return (grad_hidden, token_loss)


def solution(mesh):
    fine = Mesh(mesh.devices.reshape(4, 2, 2, 2, 8), ("x", "yh", "yl", "c", "z"))
    in_specs = (P(DP, None), P(DP, None), P(DP, "z"), P("z", DP), P(DP))
    out_specs = (P(DP, None), P(DP))
    return jax.shard_map(local, mesh=fine, in_specs=in_specs, out_specs=out_specs, check_vma=False)
```

```python
import jax
import jax.numpy as jnp
from jax import lax
from jax.experimental import pallas as pl
from jax.experimental.pallas import tpu as pltpu
from jax.sharding import Mesh, PartitionSpec as P

ce_weight = 0.5
digit = 64
lanes = 128
big_vmem = 56 * 2**20
XYH = ("x", "yh")
XY = ("x", "yh", "yl")
DP = ("x", "yh", "yl", "c")


def swap_cores(value):
    return lax.ppermute(value, "c", [(0, 1), (1, 0)])


def in_core_order(mine, other, axis):
    first = lax.axis_index("c") == 0
    return jnp.concatenate(
        [jnp.where(first, mine, other), jnp.where(first, other, mine)], axis=axis
    )


def exchange(value, axes):
    return lax.all_to_all(value, axes, 0, 0, tiled=True)


def spread(value, axes):
    count = lax.axis_size(axes)
    return exchange(jnp.broadcast_to(value[None], (count,) + value.shape), axes)


def merge(stats):
    student_tops, teacher_tops = stats[:, 0], stats[:, 1]
    student_top = jnp.max(student_tops, axis=0)
    teacher_top = jnp.max(teacher_tops, axis=0)
    student_scale = jnp.exp(student_tops - student_top)
    teacher_scale = jnp.exp(teacher_tops - teacher_top)
    return jnp.stack(
        [
            student_top,
            teacher_top,
            jnp.sum(stats[:, 2] * student_scale, axis=0),
            jnp.sum(stats[:, 3] * teacher_scale, axis=0),
            jnp.sum(stats[:, 4] * student_scale, axis=0),
            jnp.sum(stats[:, 5], axis=0),
        ]
    )


def teacher_kernel(rows_ref, cols_ref, out_ref):
    planes, pair, some, unit = out_ref.shape
    part = jnp.dot(rows_ref[...], cols_ref[...], preferred_element_type=jnp.float32)
    for j in range(pair):
        out_ref[:, j] = part[:, j * unit : (j + 1) * unit].reshape(planes, some, unit)


def teacher_partial(rows, head, planes, unit):
    depth, width = head.shape
    tokens = rows.shape[0]
    units = width // unit
    return pl.pallas_call(
        teacher_kernel,
        grid=(units // 2,),
        in_specs=[
            pl.BlockSpec((tokens, depth), lambda j: (0, 0)),
            pl.BlockSpec((depth, 2 * unit), lambda j: (0, j)),
        ],
        out_specs=pl.BlockSpec((planes, 2, tokens // planes, unit), lambda j: (0, j, 0, 0)),
        out_shape=jax.ShapeDtypeStruct((planes, units, tokens // planes, unit), jnp.float32),
        compiler_params=pltpu.CompilerParams(vmem_limit_bytes=big_vmem),
    )(rows, head)


def regroup_kernel(head_ref, out_ref):
    unit = out_ref.shape[4]
    for j in range(out_ref.shape[0]):
        out_ref[j, 0, 0] = head_ref[:, j * unit : (j + 1) * unit]


def regroup(head, units, unit):
    rows, width = head.shape
    return pl.pallas_call(
        regroup_kernel,
        grid=(2, 2),
        in_specs=[pl.BlockSpec((rows, width // 4), lambda yl, core: (0, yl * 2 + core))],
        out_specs=pl.BlockSpec(
            (units, 1, 1, rows, unit), lambda yl, core: (0, yl, core, 0, 0)
        ),
        out_shape=jax.ShapeDtypeStruct((units, 2, 2, rows, unit), head.dtype),
        compiler_params=pltpu.CompilerParams(vmem_limit_bytes=32 * 2**20),
    )(head)


def student_kernel(core_ref, rows_ref, own_ref, pair_ref, mine_ref, other_ref):
    depth, unit = rows_ref.shape[1], mine_ref.shape[1]
    for cols_ref, out_ref in ((own_ref, mine_ref), (pair_ref, other_ref)):
        cols = cols_ref[:, 0].reshape(depth, unit)
        out_ref[...] = jnp.dot(rows_ref[...], cols, preferred_element_type=jnp.float32)


def student_partial(core, rows, cols):
    tokens, depth = rows.shape
    groups, _, part, unit = cols.shape
    block = 128
    half = jax.ShapeDtypeStruct((tokens, unit), jnp.float32)
    return pl.pallas_call(
        student_kernel,
        grid_spec=pltpu.PrefetchScalarGridSpec(
            num_scalar_prefetch=1,
            grid=(tokens // block,),
            in_specs=[
                pl.BlockSpec((block, depth), lambda i, core: (i, 0)),
                pl.BlockSpec((groups, 1, part, unit), lambda i, core: (0, core[0], 0, 0)),
                pl.BlockSpec((groups, 1, part, unit), lambda i, core: (0, 1 - core[0], 0, 0)),
            ],
            out_specs=[pl.BlockSpec((block, unit), lambda i, core: (i, 0))] * 2,
        ),
        out_shape=[half, half],
        compiler_params=pltpu.CompilerParams(vmem_limit_bytes=32 * 2**20),
    )(core, rows, cols, cols)


def grad_kernel(core_ref, own_grad_ref, pair_grad_ref, own_ref, pair_ref, out_ref):
    total = None
    for grad_ref, cols_ref in ((own_grad_ref, own_ref), (pair_grad_ref, pair_ref)):
        cols = cols_ref[:, 0].reshape(out_ref.shape[1], grad_ref.shape[1])
        term = lax.dot_general(
            grad_ref[...], cols, (((1,), (1,)), ((), ())), preferred_element_type=jnp.float32
        )
        total = term if total is None else total + term
    out_ref[...] = total.astype(out_ref.dtype)


def grad_partial(core, own_grad, pair_grad, cols):
    tokens, unit = own_grad.shape
    groups, _, part, _ = cols.shape
    block = 4
    return pl.pallas_call(
        grad_kernel,
        grid_spec=pltpu.PrefetchScalarGridSpec(
            num_scalar_prefetch=1,
            grid=(groups // block,),
            in_specs=[
                pl.BlockSpec((tokens, unit), lambda i, core: (0, 0)),
                pl.BlockSpec((tokens, unit), lambda i, core: (0, 0)),
                pl.BlockSpec((block, 1, part, unit), lambda i, core: (i, core[0], 0, 0)),
                pl.BlockSpec((block, 1, part, unit), lambda i, core: (i, 1 - core[0], 0, 0)),
            ],
            out_specs=pl.BlockSpec((tokens, block * part), lambda i, core: (0, i)),
        ),
        out_shape=jax.ShapeDtypeStruct((tokens, groups * part), jnp.bfloat16),
        compiler_params=pltpu.CompilerParams(vmem_limit_bytes=32 * 2**20),
    )(core, own_grad, pair_grad, cols, cols)


def local(student_hidden, teacher_hidden, student_head, teacher_head, sampled_ids):
    core = lax.axis_index("c")
    core_id = core.reshape(1).astype(jnp.int32)
    plane = lax.axis_index("z")
    tok, width = student_hidden.shape
    xy_count = lax.axis_size(XY)
    z_count = lax.axis_size("z")
    row_part = student_head.shape[0]
    unit = teacher_head.shape[1] // z_count
    depth = teacher_head.shape[0]
    half = width // 2

    teacher_slice = lax.dynamic_slice_in_dim(teacher_hidden, plane * depth, depth, 1)
    digits = jnp.stack(
        [sampled_ids // (digit * digit), sampled_ids // digit % digit, sampled_ids % digit], axis=1
    ).astype(jnp.bfloat16)
    digits = jnp.pad(digits, ((0, 0), (0, lanes - 3)))
    shared = jnp.concatenate([teacher_slice, digits], axis=1)
    pair = in_core_order(shared, swap_cores(shared), 0)
    student_hidden, student_head, pair = lax.optimization_barrier(
        (student_hidden, student_head, pair)
    )
    gathered = spread(pair, XY).reshape(-1, depth + lanes)
    tokens = gathered.shape[0]
    some = tokens // z_count
    id_digits = gathered[:, depth : depth + 3].astype(jnp.int32)
    all_ids = (id_digits[:, 0] * digit + id_digits[:, 1]) * digit + id_digits[:, 2]

    parts = regroup(student_head, z_count, unit).reshape(xy_count, 2, row_part, unit)
    by_core = student_hidden.reshape(tok, xy_count, 2, row_part)
    even = by_core[:, :, 0].reshape(tok, half)
    odd = by_core[:, :, 1].reshape(tok, half)
    received = swap_cores(jnp.where(core == 0, odd, even))
    student_pair = in_core_order(jnp.where(core == 0, even, odd), received, 0)
    copies = jnp.broadcast_to(student_pair[None], (xy_count,) + student_pair.shape)

    gathered, parts, copies = lax.optimization_barrier((gathered, parts, copies))
    teacher_part = teacher_partial(gathered, teacher_head, z_count, unit)
    parts, copies, teacher_part = lax.optimization_barrier((parts, copies, teacher_part))
    teacher_own = lax.psum_scatter(teacher_part, "z", scatter_dimension=0, tiled=False)

    student_rows = exchange(copies, XY).reshape(tokens, half)
    student_cols = exchange(parts, XY)
    mine, other = student_partial(core_id, student_rows, student_cols)
    student_logits = mine + swap_cores(other)

    teacher_own, _ = lax.optimization_barrier((teacher_own, student_cols))
    teacher_logits = exchange(exchange(teacher_own, XYH), "z").reshape(tokens, unit)

    xyh = lax.axis_index("x") * 2 + lax.axis_index("yh")
    owner = (plane * 2 + lax.axis_index("yl")) * 2 + core
    column_ids = (owner * z_count + xyh) * unit + jnp.arange(unit, dtype=jnp.int32)
    hit_mask = (column_ids[None, :] == all_ids[:, None]).astype(jnp.float32)

    logit_gap = student_logits - teacher_logits
    student_top = jnp.max(student_logits, axis=1)
    teacher_top = jnp.max(teacher_logits, axis=1)
    student_exp = jnp.exp(student_logits - student_top[:, None])
    teacher_exp = jnp.exp(teacher_logits - teacher_top[:, None])
    stats = jnp.stack(
        [
            student_top,
            teacher_top,
            jnp.sum(student_exp, axis=1),
            jnp.sum(teacher_exp, axis=1),
            jnp.sum(student_exp * logit_gap, axis=1),
            jnp.sum(hit_mask * student_logits, axis=1),
        ]
    )
    stats = merge(jnp.stack([stats, swap_cores(stats)]))
    stats = merge(spread(stats, XY))
    stats = merge(spread(stats, "z"))
    student_norm = stats[0] + jnp.log(stats[2])
    teacher_norm = stats[1] + jnp.log(stats[3])
    expected_gap = stats[4] / stats[2]
    divergence = expected_gap - student_norm + teacher_norm
    every_loss = divergence + ce_weight * (student_norm - stats[5])
    token_loss = lax.dynamic_slice_in_dim(every_loss, lax.axis_index(DP) * tok, tok, 0)

    student_prob = jnp.exp(student_logits - student_norm[:, None])
    logit_grad = (
        student_prob * (logit_gap - expected_gap[:, None])
        + ce_weight * (student_prob - hit_mask)
    ).astype(jnp.bfloat16)
    grad_part = grad_partial(core_id, logit_grad, swap_cores(logit_grad), student_cols)
    grad_part = grad_part.reshape(xy_count, 2 * tok, half)
    plane_sum = jnp.sum(exchange(grad_part, XY).astype(jnp.float32), axis=0)
    plane_part = plane_sum.astype(jnp.bfloat16).reshape(z_count, -1, half)
    total = jnp.sum(exchange(plane_part, "z").astype(jnp.float32), axis=0).astype(jnp.bfloat16)

    grads = spread(total, "z").reshape(2, tok, half)
    mine = jnp.where(core == 0, grads[0], grads[1])
    other = swap_cores(jnp.where(core == 0, grads[1], grads[0]))
    grad_hidden = in_core_order(
        mine.reshape(tok, xy_count, 1, row_part), other.reshape(tok, xy_count, 1, row_part), 2
    ).reshape(tok, width)
    return (grad_hidden, token_loss)


def solution(mesh):
    fine = Mesh(mesh.devices.reshape(4, 2, 2, 2, 8), ("x", "yh", "yl", "c", "z"))
    in_specs = (P(DP, None), P(DP, None), P(DP, "z"), P("z", DP), P(DP))
    out_specs = (P(DP, None), P(DP))
    return jax.shard_map(local, mesh=fine, in_specs=in_specs, out_specs=out_specs, check_vma=False)
```

```python
import jax
import jax.numpy as jnp
from jax import lax
from jax.experimental import pallas as pl
from jax.experimental.pallas import tpu as pltpu
from jax.sharding import Mesh, PartitionSpec as P

ce_weight = 0.5
digit = 64
lanes = 128
big_vmem = 56 * 2**20
XY = "xy"
DP = ("xy", "c")
near_groups = [
    [4 * x + y for x in range(4) for y in pair] for pair in ((0, 3), (1, 2))
]


def swap_cores(value):
    return lax.ppermute(value, "c", [(0, 1), (1, 0)])


def in_core_order(mine, other, axis):
    first = lax.axis_index("c") == 0
    return jnp.concatenate(
        [jnp.where(first, mine, other), jnp.where(first, other, mine)], axis=axis
    )


def exchange(value, axes):
    return lax.all_to_all(value, axes, 0, 0, tiled=True)


def spread(value, axes):
    count = lax.axis_size(axes)
    return exchange(jnp.broadcast_to(value[None], (count,) + value.shape), axes)


def merge(stats):
    student_tops, teacher_tops = stats[:, 0], stats[:, 1]
    student_top = jnp.max(student_tops, axis=0)
    teacher_top = jnp.max(teacher_tops, axis=0)
    student_scale = jnp.exp(student_tops - student_top)
    teacher_scale = jnp.exp(teacher_tops - teacher_top)
    return jnp.stack(
        [
            student_top,
            teacher_top,
            jnp.sum(stats[:, 2] * student_scale, axis=0),
            jnp.sum(stats[:, 3] * teacher_scale, axis=0),
            jnp.sum(stats[:, 4] * student_scale, axis=0),
            jnp.sum(stats[:, 5], axis=0),
        ]
    )


def teacher_regroup_kernel(head_ref, out_ref):
    unit = out_ref.shape[2]
    for j in range(out_ref.shape[0]):
        out_ref[j] = head_ref[:, j * unit : (j + 1) * unit]


def teacher_regroup(head, unit):
    depth, width = head.shape
    units = width // unit
    block = units // 2
    return pl.pallas_call(
        teacher_regroup_kernel,
        grid=(units // block,),
        in_specs=[pl.BlockSpec((depth, block * unit), lambda j: (0, j))],
        out_specs=pl.BlockSpec((block, depth, unit), lambda j: (j, 0, 0)),
        out_shape=jax.ShapeDtypeStruct((units, depth, unit), head.dtype),
        compiler_params=pltpu.CompilerParams(vmem_limit_bytes=big_vmem),
    )(head)


def teacher_kernel(rows_ref, cols_ref, out_ref):
    unit = out_ref.shape[2]
    for j in range(0, out_ref.shape[0], 2):
        cols = jnp.concatenate([cols_ref[j], cols_ref[j + 1]], axis=1)
        part = jnp.dot(rows_ref[...], cols, preferred_element_type=jnp.float32)
        out_ref[j] = part[:, :unit]
        out_ref[j + 1] = part[:, unit:]


def teacher_partial(rows, cols, depth):
    units, _, unit = cols.shape
    tokens = rows.shape[0]
    block = units // 2
    return pl.pallas_call(
        teacher_kernel,
        grid=(units // block,),
        in_specs=[
            pl.BlockSpec((tokens, depth), lambda j: (0, 0)),
            pl.BlockSpec((block, depth, unit), lambda j: (j, 0, 0)),
        ],
        out_specs=pl.BlockSpec((block, tokens, unit), lambda j: (j, 0, 0)),
        out_shape=jax.ShapeDtypeStruct((units, tokens, unit), jnp.float32),
        compiler_params=pltpu.CompilerParams(vmem_limit_bytes=big_vmem),
    )(rows, cols)


def regroup_kernel(odd_ref, low_ref, high_ref, out_ref):
    unit = out_ref.shape[4]
    odd = odd_ref[0]
    for half, head_ref in enumerate((low_ref, high_ref)):
        for j in range(out_ref.shape[0]):
            row = 1 - odd if half != j % 2 else odd
            out_ref[j, row, 0] = head_ref[:, j * unit : (j + 1) * unit]


def regroup(odd, head, units, unit):
    rows, width = head.shape
    return pl.pallas_call(
        regroup_kernel,
        grid_spec=pltpu.PrefetchScalarGridSpec(
            num_scalar_prefetch=1,
            grid=(2,),
            in_specs=[
                pl.BlockSpec((rows, width // 4), lambda core, odd: (0, core)),
                pl.BlockSpec((rows, width // 4), lambda core, odd: (0, 2 + core)),
            ],
            out_specs=pl.BlockSpec(
                (units, 2, 1, rows, unit), lambda core, odd: (0, 0, core, 0, 0)
            ),
        ),
        out_shape=jax.ShapeDtypeStruct((units, 2, 2, rows, unit), head.dtype),
        compiler_params=pltpu.CompilerParams(vmem_limit_bytes=32 * 2**20),
    )(odd, head, head)


def student_kernel(core_ref, rows_ref, own_ref, pair_ref, mine_ref, other_ref):
    unit = mine_ref.shape[1]
    rows = jnp.concatenate([rows_ref[k] for k in range(rows_ref.shape[0])], axis=1)
    for cols_ref, out_ref in ((own_ref, mine_ref), (pair_ref, other_ref)):
        cols = cols_ref[:, 0].reshape(rows.shape[1], unit)
        out_ref[...] = jnp.dot(rows, cols, preferred_element_type=jnp.float32)


def student_partial(core, rows, cols):
    slices, tokens, depth = rows.shape
    groups, _, part, unit = cols.shape
    block = 128
    half = jax.ShapeDtypeStruct((tokens, unit), jnp.float32)
    return pl.pallas_call(
        student_kernel,
        grid_spec=pltpu.PrefetchScalarGridSpec(
            num_scalar_prefetch=1,
            grid=(tokens // block,),
            in_specs=[
                pl.BlockSpec((slices, block, depth), lambda i, core: (0, i, 0)),
                pl.BlockSpec((groups, 1, part, unit), lambda i, core: (0, core[0], 0, 0)),
                pl.BlockSpec((groups, 1, part, unit), lambda i, core: (0, 1 - core[0], 0, 0)),
            ],
            out_specs=[pl.BlockSpec((block, unit), lambda i, core: (i, 0))] * 2,
        ),
        out_shape=[half, half],
        compiler_params=pltpu.CompilerParams(vmem_limit_bytes=32 * 2**20),
    )(core, rows, cols, cols)


def grad_kernel(core_ref, own_grad_ref, pair_grad_ref, own_ref, pair_ref, out_ref):
    total = None
    for grad_ref, cols_ref in ((own_grad_ref, own_ref), (pair_grad_ref, pair_ref)):
        cols = cols_ref[:, 0].reshape(out_ref.shape[1], grad_ref.shape[1])
        term = lax.dot_general(
            grad_ref[...], cols, (((1,), (1,)), ((), ())), preferred_element_type=jnp.float32
        )
        total = term if total is None else total + term
    out_ref[...] = total.astype(out_ref.dtype)


def grad_partial(core, own_grad, pair_grad, cols):
    tokens, unit = own_grad.shape
    groups, _, part, _ = cols.shape
    block = 4
    return pl.pallas_call(
        grad_kernel,
        grid_spec=pltpu.PrefetchScalarGridSpec(
            num_scalar_prefetch=1,
            grid=(groups // block,),
            in_specs=[
                pl.BlockSpec((tokens, unit), lambda i, core: (0, 0)),
                pl.BlockSpec((tokens, unit), lambda i, core: (0, 0)),
                pl.BlockSpec((block, 1, part, unit), lambda i, core: (i, core[0], 0, 0)),
                pl.BlockSpec((block, 1, part, unit), lambda i, core: (i, 1 - core[0], 0, 0)),
            ],
            out_specs=pl.BlockSpec((tokens, block * part), lambda i, core: (0, i)),
        ),
        out_shape=jax.ShapeDtypeStruct((tokens, groups * part), jnp.bfloat16),
        compiler_params=pltpu.CompilerParams(vmem_limit_bytes=32 * 2**20),
    )(core, own_grad, pair_grad, cols, cols)


def local(student_hidden, teacher_hidden, student_head, teacher_head, sampled_ids):
    core = lax.axis_index("c")
    core_id = core.reshape(1).astype(jnp.int32)
    plane = lax.axis_index("z")
    tok, width = student_hidden.shape
    xy_count = lax.axis_size(XY)
    z_count = lax.axis_size("z")
    row_part = student_head.shape[0]
    unit = teacher_head.shape[1] // z_count
    depth = teacher_head.shape[0]
    half = width // 2

    share = half // z_count
    student_slice = lax.dynamic_slice_in_dim(student_hidden, plane * 2 * share, 2 * share, 1)
    by_core = student_slice.reshape(tok, -1, 2, row_part)
    even = by_core[:, :, 0].reshape(tok, share)
    odd = by_core[:, :, 1].reshape(tok, share)
    keep = jnp.where(core == 0, even, odd)
    give = jnp.where(core == 0, odd, even)
    teacher_slice = lax.dynamic_slice_in_dim(teacher_hidden, plane * depth, depth, 1)
    received = swap_cores(jnp.concatenate([teacher_slice, give], axis=1))
    pair = in_core_order(jnp.concatenate([teacher_slice, keep], axis=1), received, 0)
    teacher_head, student_head, sampled_ids, pair = lax.optimization_barrier(
        (teacher_head, student_head, sampled_ids, pair)
    )
    gathered = spread(pair, XY).reshape(-1, depth + share)
    tokens = gathered.shape[0]

    teacher_parts = teacher_regroup(teacher_head, unit)
    odd_plane = lax.rem(plane, 2)
    parts = regroup(odd_plane.reshape(1).astype(jnp.int32), student_head, z_count, unit)
    parts = parts.reshape(xy_count, 2, row_part, unit)
    digits = jnp.stack(
        [sampled_ids // (digit * digit), sampled_ids // digit % digit, sampled_ids % digit], axis=1
    ).astype(jnp.bfloat16)
    digits = jnp.pad(digits, ((0, 0), (0, lanes - 3)))
    digits = in_core_order(digits, swap_cores(digits), 0)
    share_rows = gathered[:, depth:]
    teacher_parts, gathered, share_rows, parts, digits = lax.optimization_barrier(
        (teacher_parts, gathered, share_rows, parts, digits)
    )

    student_rows = lax.all_gather(share_rows, "z", axis=0, tiled=False)
    teacher_cols = lax.all_to_all(
        teacher_parts, XY, 0, 0, axis_index_groups=near_groups, tiled=True
    )
    teacher_part = teacher_partial(gathered, teacher_cols, depth)

    parts, teacher_part = lax.optimization_barrier((parts, teacher_part))
    teacher_logits = lax.psum_scatter(teacher_part, "z", scatter_dimension=0, tiled=False)
    student_cols = exchange(parts, XY)
    digits, core_id, place, student_cols = lax.optimization_barrier(
        (digits, core_id, lax.axis_index(XY), student_cols)
    )
    id_digits = spread(digits, XY).reshape(tokens, lanes)[:, :3].astype(jnp.int32)
    all_ids = (id_digits[:, 0] * digit + id_digits[:, 1]) * digit + id_digits[:, 2]
    mine, other = student_partial(core_id, student_rows, student_cols)
    student_logits = mine + swap_cores(other)

    row = lax.rem(place, 4)
    xyh = place // 2
    near = lax.rem(row // 2 + row, 2)
    owner = (plane * 2 + lax.rem(near + plane, 2)) * 2 + core
    column_ids = (owner * z_count + xyh) * unit + jnp.arange(unit, dtype=jnp.int32)
    hit_mask = (column_ids[None, :] == all_ids[:, None]).astype(jnp.float32)

    logit_gap = student_logits - teacher_logits
    student_top = jnp.max(student_logits, axis=1)
    teacher_top = jnp.max(teacher_logits, axis=1)
    student_exp = jnp.exp(student_logits - student_top[:, None])
    teacher_exp = jnp.exp(teacher_logits - teacher_top[:, None])
    stats = jnp.stack(
        [
            student_top,
            teacher_top,
            jnp.sum(student_exp, axis=1),
            jnp.sum(teacher_exp, axis=1),
            jnp.sum(student_exp * logit_gap, axis=1),
            jnp.sum(hit_mask * student_logits, axis=1),
        ]
    )
    stats = merge(jnp.stack([stats, swap_cores(stats)]))
    stats = merge(spread(stats, XY))
    stats = merge(spread(stats, "z"))
    student_norm = stats[0] + jnp.log(stats[2])
    teacher_norm = stats[1] + jnp.log(stats[3])
    expected_gap = stats[4] / stats[2]
    divergence = expected_gap - student_norm + teacher_norm
    every_loss = divergence + ce_weight * (student_norm - stats[5])
    token_loss = lax.dynamic_slice_in_dim(every_loss, lax.axis_index(DP) * tok, tok, 0)

    student_prob = jnp.exp(student_logits - student_norm[:, None])
    logit_grad = (
        student_prob * (logit_gap - expected_gap[:, None])
        + ce_weight * (student_prob - hit_mask)
    ).astype(jnp.bfloat16)
    grad_part = grad_partial(core_id, logit_grad, swap_cores(logit_grad), student_cols)
    grad_part = grad_part.reshape(xy_count, 2 * tok, half)
    plane_sum = jnp.sum(exchange(grad_part, XY).astype(jnp.float32), axis=0)
    plane_part = plane_sum.astype(jnp.bfloat16).reshape(z_count, -1, half)
    total = jnp.sum(exchange(plane_part, "z").astype(jnp.float32), axis=0).astype(jnp.bfloat16)

    grads = spread(total, "z").reshape(2, tok, half)
    mine = jnp.where(core == 0, grads[0], grads[1])
    other = swap_cores(jnp.where(core == 0, grads[1], grads[0]))
    grad_hidden = in_core_order(
        mine.reshape(tok, xy_count, 1, row_part), other.reshape(tok, xy_count, 1, row_part), 2
    ).reshape(tok, width)
    return (grad_hidden, token_loss)


def solution(mesh):
    fine = Mesh(mesh.devices.reshape(16, 2, 8), ("xy", "c", "z"))
    in_specs = (P(DP, None), P(DP, None), P(DP, "z"), P("z", DP), P(DP))
    out_specs = (P(DP, None), P(DP))
    return jax.shard_map(local, mesh=fine, in_specs=in_specs, out_specs=out_specs, check_vma=False)
```

```python
import jax
import jax.numpy as jnp
from jax import lax
from jax.experimental import pallas as pl
from jax.experimental.pallas import tpu as pltpu
from jax.sharding import Mesh, PartitionSpec as P

ce_weight = 0.5
digit = 64
lanes = 128
stat_rows = 8
big_vmem = 56 * 2**20
XY = "xy"
DP = ("xy", "c")
near_groups = [
    [4 * x + y for x in range(4) for y in pair] for pair in ((0, 3), (1, 2))
]


def swap_cores(value):
    return lax.ppermute(value, "c", [(0, 1), (1, 0)])


def exchange(value, axes):
    return lax.all_to_all(value, axes, 0, 0, tiled=True)


def spread(value, axes):
    count = lax.axis_size(axes)
    return exchange(jnp.broadcast_to(value[None], (count,) + value.shape), axes)


def hits(info_ref, h, digits_ref, shape):
    digits = digits_ref[...].astype(jnp.float32)
    ids = (digits[:, 0:1] * digit + digits[:, 1:2]) * digit + digits[:, 2:3]
    columns = info_ref[1 + h] + lax.broadcasted_iota(jnp.int32, shape, 1)
    return columns == ids.astype(jnp.int32)


def stats_kernel(info_ref, digits_ref, student_ref, own_ref, pair_ref, out_ref):
    teacher = (own_ref, pair_ref)
    tokens, unit = own_ref.shape
    tops = [jnp.full((tokens, 1), -jnp.inf, jnp.float32)] * 2
    for h in range(2):
        tops[0] = jnp.maximum(tops[0], jnp.max(student_ref[h], axis=1, keepdims=True))
        tops[1] = jnp.maximum(tops[1], jnp.max(teacher[h][...], axis=1, keepdims=True))
    sums = [jnp.zeros((tokens, 1), jnp.float32)] * 4
    for h in range(2):
        student, other = student_ref[h], teacher[h][...]
        weight = jnp.exp(student - tops[0])
        found = jnp.where(hits(info_ref, h, digits_ref, (tokens, unit)), student, 0.0)
        terms = (weight, jnp.exp(other - tops[1]), weight * (student - other), found)
        sums = [a + jnp.sum(b, axis=1, keepdims=True) for a, b in zip(sums, terms)]
    lane = lax.broadcasted_iota(jnp.int32, (tokens, lanes), 1)
    table = jnp.zeros((tokens, lanes), jnp.float32)
    for k, column in enumerate(tops + sums):
        table = jnp.where(lane == k, column, table)
    out_ref[...] = jnp.broadcast_to(table.T[: out_ref.shape[1]], out_ref.shape)


def merged(stats):
    tops = jnp.max(stats, axis=0)
    scale = jnp.exp(stats - tops[None])
    row = lax.broadcasted_iota(jnp.int32, stats.shape, 1)
    weight = jnp.where((row == 2) | (row == 4), scale[:, 0:1], 0.0)
    weight = jnp.where(row == 3, scale[:, 1:2], weight)
    weight = jnp.where(row == 5, 1.0, weight)
    total = jnp.sum(stats * weight, axis=0)
    return jnp.where(lax.broadcasted_iota(jnp.int32, tops.shape, 0) < 2, tops, total)


def merge_kernel(stats_ref, out_ref):
    out_ref[...] = jnp.broadcast_to(merged(stats_ref[...]), out_ref.shape)


def merge(stats, copies):
    return pl.pallas_call(
        merge_kernel,
        out_shape=jax.ShapeDtypeStruct((copies,) + stats.shape[1:], jnp.float32),
    )(stats)


def local_stats(info, digits, student, teacher, pair, copies):
    tokens, unit = pair.shape
    first = lambda i, info: (0, 0)
    return pl.pallas_call(
        stats_kernel,
        grid_spec=pltpu.PrefetchScalarGridSpec(
            num_scalar_prefetch=1,
            grid=(1,),
            in_specs=[
                pl.BlockSpec(digits.shape, first),
                pl.BlockSpec(student.shape, lambda i, info: (0, 0, 0)),
                pl.BlockSpec((tokens, unit), first),
                pl.BlockSpec((tokens, unit), first),
            ],
            out_specs=pl.BlockSpec((copies, stat_rows, tokens), lambda i, info: (0, 0, 0)),
        ),
        out_shape=jax.ShapeDtypeStruct((copies, stat_rows, tokens), jnp.float32),
        compiler_params=pltpu.CompilerParams(vmem_limit_bytes=32 * 2**20),
    )(info, digits, student, teacher, pair)


def teacher_regroup_kernel(head_ref, out_ref):
    unit = out_ref.shape[2]
    for j in range(out_ref.shape[0]):
        out_ref[j] = head_ref[:, j * unit : (j + 1) * unit]


def teacher_regroup(head, unit):
    depth, width = head.shape
    units = width // unit
    block = units // 2
    return pl.pallas_call(
        teacher_regroup_kernel,
        grid=(units // block,),
        in_specs=[pl.BlockSpec((depth, block * unit), lambda j: (0, j))],
        out_specs=pl.BlockSpec((block, depth, unit), lambda j: (j, 0, 0)),
        out_shape=jax.ShapeDtypeStruct((units, depth, unit), head.dtype),
        compiler_params=pltpu.CompilerParams(vmem_limit_bytes=big_vmem),
    )(head)


def teacher_kernel(own_ref, other_ref, cols_ref, out_ref):
    unit = out_ref.shape[2]
    count = own_ref.shape[0]
    for j in range(0, out_ref.shape[0], 2):
        cols = jnp.concatenate([cols_ref[j], cols_ref[j + 1]], axis=1)
        for start, rows_ref in ((0, own_ref), (count, other_ref)):
            part = jnp.dot(rows_ref[...], cols, preferred_element_type=jnp.float32)
            out_ref[j, start : start + count] = part[:, :unit]
            out_ref[j + 1, start : start + count] = part[:, unit:]


def teacher_partial(own, other, cols):
    units, depth, unit = cols.shape
    count = own.shape[0]
    block = units // 2
    return pl.pallas_call(
        teacher_kernel,
        grid=(units // block,),
        in_specs=[
            pl.BlockSpec((count, depth), lambda j: (0, 0)),
            pl.BlockSpec((count, depth), lambda j: (0, 0)),
            pl.BlockSpec((block, depth, unit), lambda j: (j, 0, 0)),
        ],
        out_specs=pl.BlockSpec((block, 2 * count, unit), lambda j: (j, 0, 0)),
        out_shape=jax.ShapeDtypeStruct((units, 2 * count, unit), jnp.float32),
        compiler_params=pltpu.CompilerParams(vmem_limit_bytes=big_vmem),
    )(own, other, cols)


def regroup_kernel(odd_ref, low_ref, high_ref, out_ref):
    unit = out_ref.shape[4]
    odd = odd_ref[0]
    for half, head_ref in enumerate((low_ref, high_ref)):
        for j in range(out_ref.shape[0]):
            row = 1 - odd if half != j % 2 else odd
            out_ref[j, row, 0] = head_ref[:, j * unit : (j + 1) * unit]


def regroup(odd, head, units, unit):
    rows, width = head.shape
    return pl.pallas_call(
        regroup_kernel,
        grid_spec=pltpu.PrefetchScalarGridSpec(
            num_scalar_prefetch=1,
            grid=(2,),
            in_specs=[
                pl.BlockSpec((rows, width // 4), lambda core, odd: (0, core)),
                pl.BlockSpec((rows, width // 4), lambda core, odd: (0, 2 + core)),
            ],
            out_specs=pl.BlockSpec(
                (units, 2, 1, rows, unit), lambda core, odd: (0, 0, core, 0, 0)
            ),
        ),
        out_shape=jax.ShapeDtypeStruct((units, 2, 2, rows, unit), head.dtype),
        compiler_params=pltpu.CompilerParams(vmem_limit_bytes=32 * 2**20),
    )(odd, head, head)


def student_kernel(core_ref, rows_ref, own_mine, own_pair, far_mine, far_pair, out_ref, turned_ref):
    core = core_ref[0]
    slices, _, depth = rows_ref.shape
    part, unit = own_mine.shape[2], own_mine.shape[3]
    own_rows, far_rows = [], []
    for k in range(slices):
        for start in range(0, depth, 2 * part):
            near = pl.multiple_of(start + core * part, part)
            away = pl.multiple_of(start + part - core * part, part)
            own_rows.append(rows_ref[k, :, pl.ds(near, part)])
            far_rows.append(rows_ref[k, :, pl.ds(away, part)])
    own_rows = jnp.concatenate(own_rows, axis=1)
    far_rows = jnp.concatenate(far_rows, axis=1)

    @pl.when(pl.program_id(0) == 0)
    def _():
        for h, cols_ref in enumerate((own_mine, own_pair)):
            turned_ref[0, h] = cols_ref[:, 0].reshape(-1, unit).T

    @pl.when(pl.program_id(0) == 1)
    def _():
        for h, cols_ref in enumerate((far_mine, far_pair)):
            turned_ref[0, h] = cols_ref[:, 0].reshape(-1, unit).T

    for h, (own_ref, far_ref) in enumerate(((own_mine, far_mine), (own_pair, far_pair))):
        out_ref[h] = jnp.dot(
            own_rows, own_ref[:, 0].reshape(-1, unit), preferred_element_type=jnp.float32
        ) + jnp.dot(far_rows, far_ref[:, 0].reshape(-1, unit), preferred_element_type=jnp.float32)


def student_full(core, rows, own, far):
    slices, tokens, depth = rows.shape
    groups, _, part, unit = own.shape
    block = tokens // 2
    cols = (groups, 1, part, unit)
    mine = pl.BlockSpec(cols, lambda i, core: (0, core[0], 0, 0))
    pair = pl.BlockSpec(cols, lambda i, core: (0, 1 - core[0], 0, 0))
    return pl.pallas_call(
        student_kernel,
        grid_spec=pltpu.PrefetchScalarGridSpec(
            num_scalar_prefetch=1,
            grid=(tokens // block,),
            in_specs=[
                pl.BlockSpec((slices, block, depth), lambda i, core: (0, i, 0)),
                mine,
                pair,
                mine,
                pair,
            ],
            out_specs=[
                pl.BlockSpec((2, block, unit), lambda i, core: (0, i, 0)),
                pl.BlockSpec((1, 2, unit, groups * part), lambda i, core: (i, 0, 0, 0)),
            ],
        ),
        out_shape=[
            jax.ShapeDtypeStruct((2, tokens, unit), jnp.float32),
            jax.ShapeDtypeStruct((2, 2, unit, groups * part), own.dtype),
        ],
        compiler_params=pltpu.CompilerParams(vmem_limit_bytes=48 * 2**20),
    )(core, rows, own, own, far, far)


def grad_kernel(
    info_ref, stats_ref, digits_ref, student_ref, own_ref, pair_ref,
    turned_ref, out_ref, loss_ref, grad_ref,
):
    core = info_ref[0]
    unit = turned_ref.shape[2]
    tokens = out_ref.shape[0]
    part = lanes
    block = turned_ref.shape[3] // part

    @pl.when(pl.program_id(0) == 0)
    def _():
        stats = merged(stats_ref[...])
        student_norm = stats[0:1] + jnp.log(stats[2:3])
        teacher_norm = stats[1:2] + jnp.log(stats[3:4])
        gap = stats[4:5] / stats[2:3]
        loss = gap - student_norm + teacher_norm + ce_weight * (student_norm - stats[5:6])
        loss_ref[...] = jnp.broadcast_to(loss, loss_ref.shape)
        row = lax.broadcasted_iota(jnp.int32, (lanes, tokens), 0)
        table = jnp.where(row == 0, student_norm, jnp.where(row == 1, gap, 0.0)).T
        for h, teacher_ref in enumerate((own_ref, pair_ref)):
            student = student_ref[h]
            prob = jnp.exp(student - table[:, 0:1])
            found = hits(info_ref, h, digits_ref, (tokens, unit)).astype(jnp.float32)
            grad = prob * ((student - teacher_ref[...]) - table[:, 1:2])
            grad_ref[h] = (grad + ce_weight * (prob - found)).astype(grad_ref.dtype)

    for near, which in ((core, 0), (1 - core, 1)):
        total = jnp.dot(
            grad_ref[0], turned_ref[which, 0], preferred_element_type=jnp.float32
        ) + jnp.dot(grad_ref[1], turned_ref[which, 1], preferred_element_type=jnp.float32)
        total = total.astype(out_ref.dtype)
        for m in range(block):
            start = pl.multiple_of((2 * m + near) * part, part)
            out_ref[:, pl.ds(start, part)] = total[:, m * part : (m + 1) * part]


def grad_partial(info, stats, digits, student, teacher_own, teacher_pair, turned):
    _, tokens, unit = student.shape
    width = turned.shape[3]
    block = width // 4
    whole = [
        pl.BlockSpec(shape, lambda i, info, n=len(shape): (0,) * n)
        for shape in (
            stats.shape, digits.shape, student.shape, (tokens, unit), (tokens, unit)
        )
    ]
    return pl.pallas_call(
        grad_kernel,
        grid_spec=pltpu.PrefetchScalarGridSpec(
            num_scalar_prefetch=1,
            grid=(width // block,),
            in_specs=whole + [pl.BlockSpec((2, 2, unit, block), lambda i, info: (0, 0, 0, i))],
            out_specs=[
                pl.BlockSpec((tokens, 2 * block), lambda i, info: (0, i)),
                pl.BlockSpec((stat_rows, tokens), lambda i, info: (0, 0)),
            ],
            scratch_shapes=[pltpu.VMEM((2, tokens, unit), jnp.bfloat16)],
        ),
        out_shape=[
            jax.ShapeDtypeStruct((tokens, 2 * width), jnp.bfloat16),
            jax.ShapeDtypeStruct((stat_rows, tokens), jnp.float32),
        ],
        compiler_params=pltpu.CompilerParams(vmem_limit_bytes=40 * 2**20),
    )(info, stats, digits, student, teacher_own, teacher_pair, turned)


def local(student_hidden, teacher_hidden, student_head, teacher_head, sampled_ids):
    core = lax.axis_index("c")
    core_id = core.reshape(1).astype(jnp.int32)
    plane = lax.axis_index("z")
    tok, width = student_hidden.shape
    xy_count = lax.axis_size(XY)
    z_count = lax.axis_size("z")
    row_part = student_head.shape[0]
    unit = teacher_head.shape[1] // z_count
    depth = teacher_head.shape[0]
    share = width // z_count

    pay = jnp.concatenate(
        [
            lax.dynamic_slice_in_dim(teacher_hidden, plane * depth, depth, 1),
            lax.dynamic_slice_in_dim(student_hidden, plane * share, share, 1),
        ],
        axis=1,
    )
    teacher_head, student_head, sampled_ids, pay = lax.optimization_barrier(
        (teacher_head, student_head, sampled_ids, pay)
    )
    gathered = spread(pay, XY).reshape(-1, depth + share)
    tokens = gathered.shape[0]

    teacher_parts = teacher_regroup(teacher_head, unit)
    odd_plane = lax.rem(plane, 2)
    parts = regroup(odd_plane.reshape(1).astype(jnp.int32), student_head, z_count, unit)
    parts = parts.reshape(xy_count, 2, row_part, unit)
    digits = jnp.stack(
        [sampled_ids // (digit * digit), sampled_ids // digit % digit, sampled_ids % digit], axis=1
    ).astype(jnp.bfloat16)
    digits = jnp.pad(digits, ((0, 0), (0, lanes - 3)))
    teacher_other = swap_cores(gathered[:, :depth])
    share_rows = gathered[:, depth:]
    teacher_parts, gathered, teacher_other, share_rows, parts, digits = lax.optimization_barrier(
        (teacher_parts, gathered, teacher_other, share_rows, parts, digits)
    )

    student_rows = lax.all_gather(share_rows, "z", axis=0, tiled=False)
    teacher_cols = lax.all_to_all(
        teacher_parts, XY, 0, 0, axis_index_groups=near_groups, tiled=True
    )
    teacher_part = teacher_partial(gathered, teacher_other, teacher_cols)

    parts, student_rows, teacher_part = lax.optimization_barrier(
        (parts, student_rows, teacher_part)
    )
    teacher_sum = lax.psum_scatter(
        teacher_part.reshape(-1, unit), "z", scatter_dimension=0, tiled=True
    )
    own_cols = exchange(parts, XY)
    far_cols = swap_cores(own_cols)
    student_logits, turned = student_full(core_id, student_rows, own_cols, far_cols)
    digits, place, turned = lax.optimization_barrier((digits, lax.axis_index(XY), turned))
    id_digits = spread(digits, XY).reshape(tokens, lanes)
    teacher_sum, id_digits = lax.optimization_barrier((teacher_sum, id_digits))
    teacher_pair = swap_cores(teacher_sum[tokens:])

    row = lax.rem(place, 4)
    xyh = place // 2
    near = lax.rem(row // 2 + row, 2)
    cores = jnp.stack([core, 1 - core]).astype(jnp.int32)
    owner = (plane * 2 + lax.rem(near + plane, 2)) * 2 + cores
    info = jnp.concatenate([core_id, (owner * z_count + xyh) * unit])

    stats = local_stats(info, id_digits, student_logits, teacher_sum, teacher_pair, xy_count)
    stats = exchange(merge(exchange(stats, XY), z_count), "z")
    grad_part, losses = grad_partial(
        info, stats, id_digits, student_logits, teacher_sum, teacher_pair, turned
    )
    token_loss = lax.dynamic_slice_in_dim(losses[0], lax.axis_index(XY) * tok, tok, 0)
    grad_part = grad_part.reshape(xy_count, tok, width)
    plane_sum = jnp.sum(exchange(grad_part, XY).astype(jnp.float32), axis=0)
    plane_part = plane_sum.astype(jnp.bfloat16).reshape(tok, z_count, share).transpose(1, 0, 2)
    total = jnp.sum(exchange(plane_part, "z").astype(jnp.float32), axis=0).astype(jnp.bfloat16)
    final = spread(total, "z")
    grad_hidden = final.transpose(1, 0, 2).reshape(tok, width)
    return (grad_hidden, token_loss)


def solution(mesh):
    fine = Mesh(mesh.devices.reshape(16, 2, 8), ("xy", "c", "z"))
    in_specs = (P(DP, None), P(DP, None), P(DP, "z"), P("z", DP), P(DP))
    out_specs = (P(DP, None), P(DP))
    return jax.shard_map(local, mesh=fine, in_specs=in_specs, out_specs=out_specs, check_vma=False)
```

```python
import jax
import jax.numpy as jnp
from jax import lax
from jax.experimental import pallas as pl
from jax.experimental.pallas import tpu as pltpu
from jax.sharding import Mesh, PartitionSpec as P

ce_weight = 0.5
digit = 64
lanes = 128
stat_rows = 4
big_vmem = 56 * 2**20
XY = "xy"
DP = ("xy", "c")
near_groups = [
    [4 * x + y for x in range(4) for y in pair] for pair in ((0, 3), (1, 2))
]


def swap_cores(value):
    return lax.ppermute(value, "c", [(0, 1), (1, 0)])


def exchange(value, axes):
    return lax.all_to_all(value, axes, 0, 0, tiled=True)


def spread(value, axes):
    count = lax.axis_size(axes)
    return exchange(jnp.broadcast_to(value[None], (count,) + value.shape), axes)


def hits(info_ref, h, digits_ref, shape):
    digits = digits_ref[...].astype(jnp.float32)
    ids = (digits[:, 0:1] * digit + digits[:, 1:2]) * digit + digits[:, 2:3]
    columns = info_ref[1 + h] + lax.broadcasted_iota(jnp.int32, shape, 1)
    return columns == ids.astype(jnp.int32)


def stats_kernel(info_ref, digits_ref, student_ref, own_ref, pair_ref, out_ref):
    teacher = (own_ref, pair_ref)
    tokens, unit = own_ref.shape
    tops = [jnp.full((tokens, 1), -jnp.inf, jnp.float32)] * 2
    for h in range(2):
        tops[0] = jnp.maximum(tops[0], jnp.max(student_ref[h], axis=1, keepdims=True))
        tops[1] = jnp.maximum(tops[1], jnp.max(teacher[h][...], axis=1, keepdims=True))
    sums = [jnp.zeros((tokens, 1), jnp.float32)] * 4
    for h in range(2):
        student, other = student_ref[h], teacher[h][...]
        weight = jnp.exp(student - tops[0])
        found = jnp.where(hits(info_ref, h, digits_ref, (tokens, unit)), student, 0.0)
        terms = (weight, jnp.exp(other - tops[1]), weight * (student - other), found)
        sums = [a + jnp.sum(b, axis=1, keepdims=True) for a, b in zip(sums, terms)]
    lane = lax.broadcasted_iota(jnp.int32, (tokens, lanes), 1)
    table = jnp.zeros((tokens, lanes), jnp.float32)
    for k, column in zip((0, 4, 1, 5, 2, 6), tops + sums):
        table = jnp.where(lane == k, column, table)
    table = table.T
    table = jnp.concatenate([table[:stat_rows], table[stat_rows : 2 * stat_rows]], axis=1)
    out_ref[...] = jnp.broadcast_to(table, out_ref.shape)


def merged(stats):
    half = stats.shape[2] // 2
    tops = jnp.max(stats[:, 0], axis=0, keepdims=True)
    scale = jnp.exp(stats[:, 0] - tops)
    sums = jnp.sum(stats[:, 1] * scale, axis=0, keepdims=True)
    cross = jnp.sum(stats[:, 2, :half] * scale[:, :half], axis=0, keepdims=True)
    picked = jnp.sum(stats[:, 2, half:], axis=0, keepdims=True)
    return tops, sums, cross, picked


def merge(stats):
    tops, sums, cross, picked = merged(stats)
    last = jnp.concatenate([cross, picked], axis=1)
    return jnp.concatenate([tops, sums, last, jnp.zeros_like(last)], axis=0)


def local_stats(info, digits, student, teacher, pair, copies):
    tokens, unit = pair.shape
    first = lambda i, info: (0, 0)
    return pl.pallas_call(
        stats_kernel,
        grid_spec=pltpu.PrefetchScalarGridSpec(
            num_scalar_prefetch=1,
            grid=(1,),
            in_specs=[
                pl.BlockSpec(digits.shape, first),
                pl.BlockSpec(student.shape, lambda i, info: (0, 0, 0)),
                pl.BlockSpec((tokens, unit), first),
                pl.BlockSpec((tokens, unit), first),
            ],
            out_specs=pl.BlockSpec((copies, stat_rows, 2 * tokens), lambda i, info: (0, 0, 0)),
        ),
        out_shape=jax.ShapeDtypeStruct((copies, stat_rows, 2 * tokens), jnp.float32),
        compiler_params=pltpu.CompilerParams(vmem_limit_bytes=32 * 2**20),
    )(info, digits, student, teacher, pair)


def teacher_regroup_kernel(head_ref, out_ref):
    unit = out_ref.shape[2]
    for j in range(out_ref.shape[0]):
        out_ref[j] = head_ref[:, j * unit : (j + 1) * unit]


def teacher_regroup(head, unit):
    depth, width = head.shape
    units = width // unit
    block = units // 2
    return pl.pallas_call(
        teacher_regroup_kernel,
        grid=(units // block,),
        in_specs=[pl.BlockSpec((depth, block * unit), lambda j: (0, j))],
        out_specs=pl.BlockSpec((block, depth, unit), lambda j: (j, 0, 0)),
        out_shape=jax.ShapeDtypeStruct((units, depth, unit), head.dtype),
        compiler_params=pltpu.CompilerParams(vmem_limit_bytes=big_vmem),
    )(head)


def teacher_kernel(own_ref, other_ref, cols_ref, out_ref):
    unit = out_ref.shape[2]
    count = own_ref.shape[0]
    for j in range(0, out_ref.shape[0], 2):
        cols = jnp.concatenate([cols_ref[j], cols_ref[j + 1]], axis=1)
        for start, rows_ref in ((0, own_ref), (count, other_ref)):
            part = jnp.dot(rows_ref[...], cols, preferred_element_type=jnp.float32)
            out_ref[j, start : start + count] = part[:, :unit]
            out_ref[j + 1, start : start + count] = part[:, unit:]


def teacher_partial(own, other, cols):
    units, depth, unit = cols.shape
    count = own.shape[0]
    block = units // 2
    return pl.pallas_call(
        teacher_kernel,
        grid=(units // block,),
        in_specs=[
            pl.BlockSpec((count, depth), lambda j: (0, 0)),
            pl.BlockSpec((count, depth), lambda j: (0, 0)),
            pl.BlockSpec((block, depth, unit), lambda j: (j, 0, 0)),
        ],
        out_specs=pl.BlockSpec((block, 2 * count, unit), lambda j: (j, 0, 0)),
        out_shape=jax.ShapeDtypeStruct((units, 2 * count, unit), jnp.float32),
        compiler_params=pltpu.CompilerParams(vmem_limit_bytes=big_vmem),
    )(own, other, cols)


def regroup_kernel(odd_ref, low_ref, high_ref, out_ref):
    unit = out_ref.shape[4]
    odd = odd_ref[0]
    for half, head_ref in enumerate((low_ref, high_ref)):
        for j in range(out_ref.shape[0]):
            row = 1 - odd if half != j % 2 else odd
            out_ref[j, row, 0] = head_ref[:, j * unit : (j + 1) * unit]


def regroup(odd, head, units, unit):
    rows, width = head.shape
    return pl.pallas_call(
        regroup_kernel,
        grid_spec=pltpu.PrefetchScalarGridSpec(
            num_scalar_prefetch=1,
            grid=(2,),
            in_specs=[
                pl.BlockSpec((rows, width // 4), lambda core, odd: (0, core)),
                pl.BlockSpec((rows, width // 4), lambda core, odd: (0, 2 + core)),
            ],
            out_specs=pl.BlockSpec(
                (units, 2, 1, rows, unit), lambda core, odd: (0, 0, core, 0, 0)
            ),
        ),
        out_shape=jax.ShapeDtypeStruct((units, 2, 2, rows, unit), head.dtype),
        compiler_params=pltpu.CompilerParams(vmem_limit_bytes=32 * 2**20),
    )(odd, head, head)


def student_kernel(core_ref, rows_ref, own_mine, own_pair, far_mine, far_pair, out_ref, turned_ref):
    core = core_ref[0]
    slices, _, depth = rows_ref.shape
    part, unit = own_mine.shape[2], own_mine.shape[3]
    own_rows, far_rows = [], []
    for k in range(slices):
        for start in range(0, depth, 2 * part):
            near = pl.multiple_of(start + core * part, part)
            away = pl.multiple_of(start + part - core * part, part)
            own_rows.append(rows_ref[k, :, pl.ds(near, part)])
            far_rows.append(rows_ref[k, :, pl.ds(away, part)])
    own_rows = jnp.concatenate(own_rows, axis=1)
    far_rows = jnp.concatenate(far_rows, axis=1)

    @pl.when(pl.program_id(0) == 0)
    def _():
        for h, cols_ref in enumerate((own_mine, own_pair)):
            turned_ref[0, h] = cols_ref[:, 0].reshape(-1, unit).T

    @pl.when(pl.program_id(0) == 1)
    def _():
        for h, cols_ref in enumerate((far_mine, far_pair)):
            turned_ref[0, h] = cols_ref[:, 0].reshape(-1, unit).T

    for h, (own_ref, far_ref) in enumerate(((own_mine, far_mine), (own_pair, far_pair))):
        out_ref[h] = jnp.dot(
            own_rows, own_ref[:, 0].reshape(-1, unit), preferred_element_type=jnp.float32
        ) + jnp.dot(far_rows, far_ref[:, 0].reshape(-1, unit), preferred_element_type=jnp.float32)


def student_full(core, rows, own, far):
    slices, tokens, depth = rows.shape
    groups, _, part, unit = own.shape
    block = tokens // 2
    cols = (groups, 1, part, unit)
    mine = pl.BlockSpec(cols, lambda i, core: (0, core[0], 0, 0))
    pair = pl.BlockSpec(cols, lambda i, core: (0, 1 - core[0], 0, 0))
    return pl.pallas_call(
        student_kernel,
        grid_spec=pltpu.PrefetchScalarGridSpec(
            num_scalar_prefetch=1,
            grid=(tokens // block,),
            in_specs=[
                pl.BlockSpec((slices, block, depth), lambda i, core: (0, i, 0)),
                mine,
                pair,
                mine,
                pair,
            ],
            out_specs=[
                pl.BlockSpec((2, block, unit), lambda i, core: (0, i, 0)),
                pl.BlockSpec((1, 2, unit, groups * part), lambda i, core: (i, 0, 0, 0)),
            ],
        ),
        out_shape=[
            jax.ShapeDtypeStruct((2, tokens, unit), jnp.float32),
            jax.ShapeDtypeStruct((2, 2, unit, groups * part), own.dtype),
        ],
        compiler_params=pltpu.CompilerParams(vmem_limit_bytes=48 * 2**20),
    )(core, rows, own, own, far, far)


def grad_kernel(
    info_ref, stats_ref, digits_ref, student_ref, own_ref, pair_ref,
    turned_ref, out_ref, loss_ref, grad_ref,
):
    core = info_ref[0]
    unit = turned_ref.shape[2]
    tokens = out_ref.shape[0]
    part = lanes
    block = turned_ref.shape[3] // part

    @pl.when(pl.program_id(0) == 0)
    def _():
        tops, sums, cross, picked = merged(stats_ref[...])
        norms = tops + jnp.log(sums)
        student_norm, teacher_norm = norms[:, :tokens], norms[:, tokens:]
        gap = cross / sums[:, :tokens]
        loss = gap - student_norm + teacher_norm + ce_weight * (student_norm - picked)
        loss_ref[...] = jnp.broadcast_to(loss, loss_ref.shape)
        row = lax.broadcasted_iota(jnp.int32, (lanes, tokens), 0)
        table = jnp.where(row == 0, student_norm, jnp.where(row == 1, gap, 0.0)).T
        for h, teacher_ref in enumerate((own_ref, pair_ref)):
            student = student_ref[h]
            prob = jnp.exp(student - table[:, 0:1])
            found = hits(info_ref, h, digits_ref, (tokens, unit)).astype(jnp.float32)
            grad = prob * ((student - teacher_ref[...]) - table[:, 1:2])
            grad_ref[h] = (grad + ce_weight * (prob - found)).astype(grad_ref.dtype)

    for near, which in ((core, 0), (1 - core, 1)):
        total = jnp.dot(
            grad_ref[0], turned_ref[which, 0], preferred_element_type=jnp.float32
        ) + jnp.dot(grad_ref[1], turned_ref[which, 1], preferred_element_type=jnp.float32)
        total = total.astype(out_ref.dtype)
        for m in range(block):
            start = pl.multiple_of((2 * m + near) * part, part)
            out_ref[:, pl.ds(start, part)] = total[:, m * part : (m + 1) * part]


def grad_partial(info, stats, digits, student, teacher_own, teacher_pair, turned):
    _, tokens, unit = student.shape
    width = turned.shape[3]
    block = width // 4
    whole = [
        pl.BlockSpec(shape, lambda i, info, n=len(shape): (0,) * n)
        for shape in (
            stats.shape, digits.shape, student.shape, (tokens, unit), (tokens, unit)
        )
    ]
    return pl.pallas_call(
        grad_kernel,
        grid_spec=pltpu.PrefetchScalarGridSpec(
            num_scalar_prefetch=1,
            grid=(width // block,),
            in_specs=whole + [pl.BlockSpec((2, 2, unit, block), lambda i, info: (0, 0, 0, i))],
            out_specs=[
                pl.BlockSpec((tokens, 2 * block), lambda i, info: (0, i)),
                pl.BlockSpec((stat_rows, tokens), lambda i, info: (0, 0)),
            ],
            scratch_shapes=[pltpu.VMEM((2, tokens, unit), jnp.bfloat16)],
        ),
        out_shape=[
            jax.ShapeDtypeStruct((tokens, 2 * width), jnp.bfloat16),
            jax.ShapeDtypeStruct((stat_rows, tokens), jnp.float32),
        ],
        compiler_params=pltpu.CompilerParams(vmem_limit_bytes=40 * 2**20),
    )(info, stats, digits, student, teacher_own, teacher_pair, turned)


def sum_kernel(parts_ref, out_ref):
    share = out_ref.shape[2]
    for k in range(out_ref.shape[0]):
        part = parts_ref[:, :, k * share : (k + 1) * share].astype(jnp.float32)
        out_ref[k] = jnp.sum(part, axis=0).astype(out_ref.dtype)


def plane_sums(parts, count):
    _, rows, width = parts.shape
    whole = pl.BlockSpec(memory_space=pltpu.VMEM)
    return pl.pallas_call(
        sum_kernel,
        in_specs=[whole],
        out_specs=whole,
        out_shape=jax.ShapeDtypeStruct((count, rows, width // count), parts.dtype),
        compiler_params=pltpu.CompilerParams(vmem_limit_bytes=16 * 2**20),
    )(parts)


def local(student_hidden, teacher_hidden, student_head, teacher_head, sampled_ids):
    core = lax.axis_index("c")
    core_id = core.reshape(1).astype(jnp.int32)
    plane = lax.axis_index("z")
    tok, width = student_hidden.shape
    xy_count = lax.axis_size(XY)
    z_count = lax.axis_size("z")
    row_part = student_head.shape[0]
    unit = teacher_head.shape[1] // z_count
    depth = teacher_head.shape[0]
    share = width // z_count

    pay = jnp.concatenate(
        [
            lax.dynamic_slice_in_dim(teacher_hidden, plane * depth, depth, 1),
            lax.dynamic_slice_in_dim(student_hidden, plane * share, share, 1),
        ],
        axis=1,
    )
    teacher_head, student_head, sampled_ids, pay = lax.optimization_barrier(
        (teacher_head, student_head, sampled_ids, pay)
    )
    gathered = spread(pay, XY).reshape(-1, depth + share)
    tokens = gathered.shape[0]

    teacher_parts = teacher_regroup(teacher_head, unit)
    odd_plane = lax.rem(plane, 2)
    parts = regroup(odd_plane.reshape(1).astype(jnp.int32), student_head, z_count, unit)
    parts = parts.reshape(xy_count, 2, row_part, unit)
    digits = jnp.stack(
        [sampled_ids // (digit * digit), sampled_ids // digit % digit, sampled_ids % digit], axis=1
    ).astype(jnp.bfloat16)
    digits = jnp.pad(digits, ((0, 0), (0, lanes - 3)))
    teacher_other = swap_cores(gathered[:, :depth])
    share_rows = gathered[:, depth:]
    teacher_parts, gathered, teacher_other, share_rows, parts, digits = lax.optimization_barrier(
        (teacher_parts, gathered, teacher_other, share_rows, parts, digits)
    )

    student_rows = lax.all_gather(share_rows, "z", axis=0, tiled=False)
    teacher_cols = lax.all_to_all(
        teacher_parts, XY, 0, 0, axis_index_groups=near_groups, tiled=True
    )
    teacher_part = teacher_partial(gathered, teacher_other, teacher_cols)

    parts, student_rows, teacher_part = lax.optimization_barrier(
        (parts, student_rows, teacher_part)
    )
    teacher_sum = lax.psum_scatter(
        teacher_part.reshape(-1, unit), "z", scatter_dimension=0, tiled=True
    )
    own_cols = exchange(parts, XY)
    far_cols = swap_cores(own_cols)
    student_logits, turned = student_full(core_id, student_rows, own_cols, far_cols)
    digits, place, turned = lax.optimization_barrier((digits, lax.axis_index(XY), turned))
    id_digits = spread(digits, XY).reshape(tokens, lanes)
    teacher_sum, id_digits = lax.optimization_barrier((teacher_sum, id_digits))
    teacher_pair = swap_cores(teacher_sum[tokens:])

    row = lax.rem(place, 4)
    xyh = place // 2
    near = lax.rem(row // 2 + row, 2)
    cores = jnp.stack([core, 1 - core]).astype(jnp.int32)
    owner = (plane * 2 + lax.rem(near + plane, 2)) * 2 + cores
    info = jnp.concatenate([core_id, (owner * z_count + xyh) * unit])

    stats = local_stats(info, id_digits, student_logits, teacher_sum, teacher_pair, xy_count)
    stats = spread(merge(exchange(stats, XY)), "z")
    grad_part, losses = grad_partial(
        info, stats, id_digits, student_logits, teacher_sum, teacher_pair, turned
    )
    token_loss = lax.dynamic_slice_in_dim(losses[0], lax.axis_index(XY) * tok, tok, 0)
    grad_part = grad_part.reshape(xy_count, tok, width)
    plane_part = plane_sums(exchange(grad_part, XY), z_count)
    total = jnp.sum(exchange(plane_part, "z").astype(jnp.float32), axis=0).astype(jnp.bfloat16)
    final = spread(total, "z")
    grad_hidden = final.transpose(1, 0, 2).reshape(tok, width)
    return (grad_hidden, token_loss)


def solution(mesh):
    fine = Mesh(mesh.devices.reshape(16, 2, 8), ("xy", "c", "z"))
    in_specs = (P(DP, None), P(DP, None), P(DP, "z"), P("z", DP), P(DP))
    out_specs = (P(DP, None), P(DP))
    return jax.shard_map(local, mesh=fine, in_specs=in_specs, out_specs=out_specs, check_vma=False)
```

```python
import jax
import jax.numpy as jnp
from jax import lax
from jax.experimental import pallas as pl
from jax.experimental.pallas import tpu as pltpu
from jax.sharding import Mesh, PartitionSpec as P

ce_weight = 0.5
digit = 64
lanes = 128
stat_rows = 4
big_vmem = 56 * 2**20
XY = "xy"
DP = ("xy", "c")
near_groups = [
    [4 * x + y for x in range(4) for y in pair] for pair in ((0, 3), (1, 2))
]


def swap_cores(value):
    return lax.ppermute(value, "c", [(0, 1), (1, 0)])


def exchange(value, axes):
    return lax.all_to_all(value, axes, 0, 0, tiled=True)


def spread(value, axes):
    count = lax.axis_size(axes)
    return exchange(jnp.broadcast_to(value[None], (count,) + value.shape), axes)


def hits(info_ref, h, digits_ref, shape):
    digits = digits_ref[...].astype(jnp.float32)
    ids = (digits[:, 0:1] * digit + digits[:, 1:2]) * digit + digits[:, 2:3]
    columns = info_ref[1 + h] + lax.broadcasted_iota(jnp.int32, shape, 1)
    return columns == ids.astype(jnp.int32)


def stats_kernel(info_ref, digits_ref, student_ref, own_ref, pair_ref, out_ref):
    teacher = (own_ref, pair_ref)
    tokens, unit = own_ref.shape
    tops = [jnp.full((tokens, 1), -jnp.inf, jnp.float32)] * 2
    for h in range(2):
        tops[0] = jnp.maximum(tops[0], jnp.max(student_ref[h], axis=1, keepdims=True))
        tops[1] = jnp.maximum(tops[1], jnp.max(teacher[h][...], axis=1, keepdims=True))
    sums = [jnp.zeros((tokens, 1), jnp.float32)] * 4
    for h in range(2):
        student, other = student_ref[h], teacher[h][...]
        weight = jnp.exp(student - tops[0])
        found = jnp.where(hits(info_ref, h, digits_ref, (tokens, unit)), student, 0.0)
        terms = (weight, jnp.exp(other - tops[1]), weight * (student - other), found)
        sums = [a + jnp.sum(b, axis=1, keepdims=True) for a, b in zip(sums, terms)]
    lane = lax.broadcasted_iota(jnp.int32, (tokens, lanes), 1)
    table = jnp.zeros((tokens, lanes), jnp.float32)
    for k, column in zip((0, 4, 1, 5, 2, 6), tops + sums):
        table = jnp.where(lane == k, column, table)
    table = table.T
    table = jnp.concatenate([table[:stat_rows], table[stat_rows : 2 * stat_rows]], axis=1)
    out_ref[...] = jnp.broadcast_to(table, out_ref.shape)


def merged(stats):
    half = stats.shape[2] // 2
    tops = jnp.max(stats[:, 0], axis=0, keepdims=True)
    scale = jnp.exp(stats[:, 0] - tops)
    sums = jnp.sum(stats[:, 1] * scale, axis=0, keepdims=True)
    cross = jnp.sum(stats[:, 2, :half] * scale[:, :half], axis=0, keepdims=True)
    picked = jnp.sum(stats[:, 2, half:], axis=0, keepdims=True)
    return tops, sums, cross, picked


def merge(stats):
    tops, sums, cross, picked = merged(stats)
    last = jnp.concatenate([cross, picked], axis=1)
    return jnp.concatenate([tops, sums, last, jnp.zeros_like(last)], axis=0)


def local_stats(info, digits, student, teacher, pair, copies):
    tokens, unit = pair.shape[0] // 2, pair.shape[1]
    first = lambda i, info: (0, 0)
    return pl.pallas_call(
        stats_kernel,
        grid_spec=pltpu.PrefetchScalarGridSpec(
            num_scalar_prefetch=1,
            grid=(1,),
            in_specs=[
                pl.BlockSpec(digits.shape, first),
                pl.BlockSpec(student.shape, lambda i, info: (0, 0, 0)),
                pl.BlockSpec((tokens, unit), first),
                pl.BlockSpec((tokens, unit), lambda i, info: (1, 0)),
            ],
            out_specs=pl.BlockSpec((copies, stat_rows, 2 * tokens), lambda i, info: (0, 0, 0)),
        ),
        out_shape=jax.ShapeDtypeStruct((copies, stat_rows, 2 * tokens), jnp.float32),
        compiler_params=pltpu.CompilerParams(vmem_limit_bytes=32 * 2**20),
    )(info, digits, student, teacher, pair)


def teacher_regroup_kernel(head_ref, out_ref):
    unit = out_ref.shape[2]
    for j in range(out_ref.shape[0]):
        out_ref[j] = head_ref[:, j * unit : (j + 1) * unit]


def teacher_regroup(head, unit):
    depth, width = head.shape
    units = width // unit
    block = units // 2
    return pl.pallas_call(
        teacher_regroup_kernel,
        grid=(units // block,),
        in_specs=[pl.BlockSpec((depth, block * unit), lambda j: (0, j))],
        out_specs=pl.BlockSpec((block, depth, unit), lambda j: (j, 0, 0)),
        out_shape=jax.ShapeDtypeStruct((units, depth, unit), head.dtype),
        compiler_params=pltpu.CompilerParams(vmem_limit_bytes=big_vmem),
    )(head)


def teacher_kernel(own_ref, other_ref, cols_ref, out_ref):
    unit = out_ref.shape[2]
    count = own_ref.shape[0]
    for j in range(0, out_ref.shape[0], 2):
        cols = jnp.concatenate([cols_ref[j], cols_ref[j + 1]], axis=1)
        for start, rows_ref in ((0, own_ref), (count, other_ref)):
            part = jnp.dot(rows_ref[...], cols, preferred_element_type=jnp.float32)
            out_ref[j, start : start + count] = part[:, :unit]
            out_ref[j + 1, start : start + count] = part[:, unit:]


def teacher_partial(own, other, cols):
    units, depth, unit = cols.shape
    count = own.shape[0]
    block = units // 2
    return pl.pallas_call(
        teacher_kernel,
        grid=(units // block,),
        in_specs=[
            pl.BlockSpec((count, depth), lambda j: (0, 0)),
            pl.BlockSpec((count, depth), lambda j: (0, 0)),
            pl.BlockSpec((block, depth, unit), lambda j: (j, 0, 0)),
        ],
        out_specs=pl.BlockSpec((block, 2 * count, unit), lambda j: (j, 0, 0)),
        out_shape=jax.ShapeDtypeStruct((units, 2 * count, unit), jnp.float32),
        compiler_params=pltpu.CompilerParams(vmem_limit_bytes=big_vmem),
    )(own, other, cols)


def regroup_kernel(odd_ref, low_ref, high_ref, out_ref):
    unit = out_ref.shape[4]
    odd = odd_ref[0]
    for half, head_ref in enumerate((low_ref, high_ref)):
        for j in range(out_ref.shape[0]):
            row = 1 - odd if half != j % 2 else odd
            out_ref[j, row, 0] = head_ref[:, j * unit : (j + 1) * unit]


def regroup(odd, head, units, unit):
    rows, width = head.shape
    return pl.pallas_call(
        regroup_kernel,
        grid_spec=pltpu.PrefetchScalarGridSpec(
            num_scalar_prefetch=1,
            grid=(2,),
            in_specs=[
                pl.BlockSpec((rows, width // 4), lambda core, odd: (0, core)),
                pl.BlockSpec((rows, width // 4), lambda core, odd: (0, 2 + core)),
            ],
            out_specs=pl.BlockSpec(
                (units, 2, 1, rows, unit), lambda core, odd: (0, 0, core, 0, 0)
            ),
        ),
        out_shape=jax.ShapeDtypeStruct((units, 2, 2, rows, unit), head.dtype),
        compiler_params=pltpu.CompilerParams(vmem_limit_bytes=32 * 2**20),
    )(odd, head, head)


def student_kernel(core_ref, rows_ref, own_mine, own_pair, far_mine, far_pair, out_ref, turned_ref):
    core = core_ref[0]
    slices, _, depth = rows_ref.shape
    part, unit = own_mine.shape[2], own_mine.shape[3]
    own_rows, far_rows = [], []
    for k in range(slices):
        for start in range(0, depth, 2 * part):
            near = pl.multiple_of(start + core * part, part)
            away = pl.multiple_of(start + part - core * part, part)
            own_rows.append(rows_ref[k, :, pl.ds(near, part)])
            far_rows.append(rows_ref[k, :, pl.ds(away, part)])
    own_rows = jnp.concatenate(own_rows, axis=1)
    far_rows = jnp.concatenate(far_rows, axis=1)

    @pl.when(pl.program_id(0) == 0)
    def _():
        for h, cols_ref in enumerate((own_mine, own_pair)):
            turned_ref[0, h] = cols_ref[:, 0].reshape(-1, unit).T

    @pl.when(pl.program_id(0) == 1)
    def _():
        for h, cols_ref in enumerate((far_mine, far_pair)):
            turned_ref[0, h] = cols_ref[:, 0].reshape(-1, unit).T

    for h, (own_ref, far_ref) in enumerate(((own_mine, far_mine), (own_pair, far_pair))):
        out_ref[h] = jnp.dot(
            own_rows, own_ref[:, 0].reshape(-1, unit), preferred_element_type=jnp.float32
        ) + jnp.dot(far_rows, far_ref[:, 0].reshape(-1, unit), preferred_element_type=jnp.float32)


def student_full(core, rows, own, far):
    slices, tokens, depth = rows.shape
    groups, _, part, unit = own.shape
    block = tokens // 2
    cols = (groups, 1, part, unit)
    mine = pl.BlockSpec(cols, lambda i, core: (0, core[0], 0, 0))
    pair = pl.BlockSpec(cols, lambda i, core: (0, 1 - core[0], 0, 0))
    return pl.pallas_call(
        student_kernel,
        grid_spec=pltpu.PrefetchScalarGridSpec(
            num_scalar_prefetch=1,
            grid=(tokens // block,),
            in_specs=[
                pl.BlockSpec((slices, block, depth), lambda i, core: (0, i, 0)),
                mine,
                pair,
                mine,
                pair,
            ],
            out_specs=[
                pl.BlockSpec((2, block, unit), lambda i, core: (0, i, 0)),
                pl.BlockSpec((1, 2, unit, groups * part), lambda i, core: (i, 0, 0, 0)),
            ],
        ),
        out_shape=[
            jax.ShapeDtypeStruct((2, tokens, unit), jnp.float32),
            jax.ShapeDtypeStruct((2, 2, unit, groups * part), own.dtype),
        ],
        compiler_params=pltpu.CompilerParams(vmem_limit_bytes=48 * 2**20),
    )(core, rows, own, own, far, far)


def grad_kernel(
    info_ref, stats_ref, digits_ref, student_ref, own_ref, pair_ref,
    turned_ref, out_ref, loss_ref, grad_ref,
):
    core = info_ref[0]
    unit = turned_ref.shape[2]
    tokens = out_ref.shape[0]
    part = lanes
    block = turned_ref.shape[3] // part

    @pl.when(pl.program_id(0) == 0)
    def _():
        tops, sums, cross, picked = merged(stats_ref[...])
        norms = tops + jnp.log(sums)
        student_norm, teacher_norm = norms[:, :tokens], norms[:, tokens:]
        gap = cross / sums[:, :tokens]
        loss = gap - student_norm + teacher_norm + ce_weight * (student_norm - picked)
        loss_ref[...] = jnp.broadcast_to(loss, loss_ref.shape)
        row = lax.broadcasted_iota(jnp.int32, (lanes, tokens), 0)
        table = jnp.where(row == 0, student_norm, jnp.where(row == 1, gap, 0.0)).T
        for h, teacher_ref in enumerate((own_ref, pair_ref)):
            student = student_ref[h]
            prob = jnp.exp(student - table[:, 0:1])
            found = hits(info_ref, h, digits_ref, (tokens, unit)).astype(jnp.float32)
            grad = prob * ((student - teacher_ref[...]) - table[:, 1:2])
            grad_ref[h] = (grad + ce_weight * (prob - found)).astype(grad_ref.dtype)

    for near, which in ((core, 0), (1 - core, 1)):
        total = jnp.dot(
            grad_ref[0], turned_ref[which, 0], preferred_element_type=jnp.float32
        ) + jnp.dot(grad_ref[1], turned_ref[which, 1], preferred_element_type=jnp.float32)
        total = total.astype(out_ref.dtype)
        for m in range(block):
            start = pl.multiple_of((2 * m + near) * part, part)
            out_ref[:, pl.ds(start, part)] = total[:, m * part : (m + 1) * part]


def grad_partial(info, stats, digits, student, teacher_own, teacher_pair, turned):
    _, tokens, unit = student.shape
    width = turned.shape[3]
    block = width // 4
    whole = [
        pl.BlockSpec(shape, lambda i, info, n=len(shape): (0,) * n)
        for shape in (
            stats.shape, digits.shape, student.shape, (tokens, unit)
        )
    ]
    whole.append(pl.BlockSpec((tokens, unit), lambda i, info: (1, 0)))
    return pl.pallas_call(
        grad_kernel,
        grid_spec=pltpu.PrefetchScalarGridSpec(
            num_scalar_prefetch=1,
            grid=(width // block,),
            in_specs=whole + [pl.BlockSpec((2, 2, unit, block), lambda i, info: (0, 0, 0, i))],
            out_specs=[
                pl.BlockSpec((tokens, 2 * block), lambda i, info: (0, i)),
                pl.BlockSpec((stat_rows, tokens), lambda i, info: (0, 0)),
            ],
            scratch_shapes=[pltpu.VMEM((2, tokens, unit), jnp.bfloat16)],
        ),
        out_shape=[
            jax.ShapeDtypeStruct((tokens, 2 * width), jnp.bfloat16),
            jax.ShapeDtypeStruct((stat_rows, tokens), jnp.float32),
        ],
        compiler_params=pltpu.CompilerParams(vmem_limit_bytes=40 * 2**20),
    )(info, stats, digits, student, teacher_own, teacher_pair, turned)


def sum_kernel(parts_ref, out_ref):
    share = out_ref.shape[2]
    for k in range(out_ref.shape[0]):
        part = parts_ref[:, :, k * share : (k + 1) * share].astype(jnp.float32)
        out_ref[k] = jnp.sum(part, axis=0).astype(out_ref.dtype)


def plane_sums(parts, count):
    _, rows, width = parts.shape
    whole = pl.BlockSpec(memory_space=pltpu.VMEM)
    return pl.pallas_call(
        sum_kernel,
        in_specs=[whole],
        out_specs=whole,
        out_shape=jax.ShapeDtypeStruct((count, rows, width // count), parts.dtype),
        compiler_params=pltpu.CompilerParams(vmem_limit_bytes=16 * 2**20),
    )(parts)


def local(student_hidden, teacher_hidden, student_head, teacher_head, sampled_ids):
    core = lax.axis_index("c")
    core_id = core.reshape(1).astype(jnp.int32)
    plane = lax.axis_index("z")
    tok, width = student_hidden.shape
    xy_count = lax.axis_size(XY)
    z_count = lax.axis_size("z")
    row_part = student_head.shape[0]
    unit = teacher_head.shape[1] // z_count
    depth = teacher_head.shape[0]
    share = width // z_count

    pay = jnp.concatenate(
        [
            lax.dynamic_slice_in_dim(teacher_hidden, plane * depth, depth, 1),
            lax.dynamic_slice_in_dim(student_hidden, plane * share, share, 1),
        ],
        axis=1,
    )
    teacher_head, student_head, sampled_ids, pay = lax.optimization_barrier(
        (teacher_head, student_head, sampled_ids, pay)
    )
    gathered = spread(pay, XY).reshape(-1, depth + share)
    tokens = gathered.shape[0]

    teacher_parts = teacher_regroup(teacher_head, unit)
    odd_plane = lax.rem(plane, 2)
    parts = regroup(odd_plane.reshape(1).astype(jnp.int32), student_head, z_count, unit)
    parts = parts.reshape(xy_count, 2, row_part, unit)
    digits = jnp.stack(
        [sampled_ids // (digit * digit), sampled_ids // digit % digit, sampled_ids % digit], axis=1
    ).astype(jnp.bfloat16)
    digits = jnp.pad(digits, ((0, 0), (0, lanes - 3)))
    teacher_other = swap_cores(gathered[:, :depth])
    share_rows = gathered[:, depth:]
    teacher_parts, gathered, teacher_other, share_rows, parts, digits = lax.optimization_barrier(
        (teacher_parts, gathered, teacher_other, share_rows, parts, digits)
    )

    student_rows = lax.all_gather(share_rows, "z", axis=0, tiled=False)
    teacher_cols = lax.all_to_all(
        teacher_parts, XY, 0, 0, axis_index_groups=near_groups, tiled=True
    )
    teacher_part = teacher_partial(gathered, teacher_other, teacher_cols)

    parts, student_rows, teacher_part = lax.optimization_barrier(
        (parts, student_rows, teacher_part)
    )
    teacher_sum = lax.psum_scatter(
        teacher_part.reshape(-1, unit), "z", scatter_dimension=0, tiled=True
    )
    own_cols = exchange(parts, XY)
    far_cols = swap_cores(own_cols)
    student_logits, turned = student_full(core_id, student_rows, own_cols, far_cols)
    digits, place, turned = lax.optimization_barrier((digits, lax.axis_index(XY), turned))
    id_digits = spread(digits, XY).reshape(tokens, lanes)
    teacher_sum, id_digits = lax.optimization_barrier((teacher_sum, id_digits))
    teacher_pair = swap_cores(teacher_sum)

    row = lax.rem(place, 4)
    xyh = place // 2
    near = lax.rem(row // 2 + row, 2)
    cores = jnp.stack([core, 1 - core]).astype(jnp.int32)
    owner = (plane * 2 + lax.rem(near + plane, 2)) * 2 + cores
    info = jnp.concatenate([core_id, (owner * z_count + xyh) * unit])

    stats = local_stats(info, id_digits, student_logits, teacher_sum, teacher_pair, xy_count)
    stats = spread(merge(exchange(stats, XY)), "z")
    grad_part, losses = grad_partial(
        info, stats, id_digits, student_logits, teacher_sum, teacher_pair, turned
    )
    token_loss = lax.dynamic_slice_in_dim(losses[0], lax.axis_index(XY) * tok, tok, 0)
    grad_part = grad_part.reshape(xy_count, tok, width)
    plane_part = plane_sums(exchange(grad_part, XY), z_count)
    total = jnp.sum(exchange(plane_part, "z").astype(jnp.float32), axis=0).astype(jnp.bfloat16)
    final = spread(total, "z")
    grad_hidden = final.transpose(1, 0, 2).reshape(tok, width)
    return (grad_hidden, token_loss)


def solution(mesh):
    fine = Mesh(mesh.devices.reshape(16, 2, 8), ("xy", "c", "z"))
    in_specs = (P(DP, None), P(DP, None), P(DP, "z"), P("z", DP), P(DP))
    out_specs = (P(DP, None), P(DP))
    return jax.shard_map(local, mesh=fine, in_specs=in_specs, out_specs=out_specs, check_vma=False)
```

```python
import jax
import jax.numpy as jnp
from jax import lax
from jax.experimental import pallas as pl
from jax.experimental.pallas import tpu as pltpu
from jax.sharding import Mesh, PartitionSpec as P

ce_weight = 0.5
digit = 64
lanes = 128
stat_rows = 4
big_vmem = 56 * 2**20
XY = "xy"
DP = ("xy", "c")
near_groups = [
    [4 * x + y for x in range(4) for y in pair] for pair in ((0, 3), (1, 2))
]


def swap_cores(value):
    return lax.ppermute(value, "c", [(0, 1), (1, 0)])


def exchange(value, axes):
    return lax.all_to_all(value, axes, 0, 0, tiled=True)


def spread(value, axes):
    count = lax.axis_size(axes)
    return exchange(jnp.broadcast_to(value[None], (count,) + value.shape), axes)


def hits(info_ref, h, digits_ref, shape):
    digits = digits_ref[...].astype(jnp.float32)
    ids = (digits[:, 0:1] * digit + digits[:, 1:2]) * digit + digits[:, 2:3]
    columns = info_ref[1 + h] + lax.broadcasted_iota(jnp.int32, shape, 1)
    return columns == ids.astype(jnp.int32)


def stats_kernel(info_ref, digits_ref, student_ref, own_ref, pair_ref, out_ref):
    teacher = (own_ref, pair_ref)
    tokens, unit = own_ref.shape
    tops = [jnp.full((tokens, 1), -jnp.inf, jnp.float32)] * 2
    for h in range(2):
        tops[0] = jnp.maximum(tops[0], jnp.max(student_ref[h], axis=1, keepdims=True))
        tops[1] = jnp.maximum(tops[1], jnp.max(teacher[h][...], axis=1, keepdims=True))
    sums = [jnp.zeros((tokens, 1), jnp.float32)] * 4
    for h in range(2):
        student, other = student_ref[h], teacher[h][...]
        weight = jnp.exp(student - tops[0])
        found = jnp.where(hits(info_ref, h, digits_ref, (tokens, unit)), student, 0.0)
        terms = (weight, jnp.exp(other - tops[1]), weight * (student - other), found)
        sums = [a + jnp.sum(b, axis=1, keepdims=True) for a, b in zip(sums, terms)]
    lane = lax.broadcasted_iota(jnp.int32, (tokens, lanes), 1)
    table = jnp.zeros((tokens, lanes), jnp.float32)
    for k, column in zip((0, 4, 1, 5, 2, 6), tops + sums):
        table = jnp.where(lane == k, column, table)
    table = table.T
    table = jnp.concatenate([table[:stat_rows], table[stat_rows : 2 * stat_rows]], axis=1)
    out_ref[...] = jnp.broadcast_to(table, out_ref.shape)


def merged(stats):
    half = stats.shape[2] // 2
    tops = jnp.max(stats[:, 0], axis=0, keepdims=True)
    scale = jnp.exp(stats[:, 0] - tops)
    sums = jnp.sum(stats[:, 1] * scale, axis=0, keepdims=True)
    cross = jnp.sum(stats[:, 2, :half] * scale[:, :half], axis=0, keepdims=True)
    picked = jnp.sum(stats[:, 2, half:], axis=0, keepdims=True)
    return tops, sums, cross, picked


def merge(stats):
    tops, sums, cross, picked = merged(stats)
    last = jnp.concatenate([cross, picked], axis=1)
    return jnp.concatenate([tops, sums, last, jnp.zeros_like(last)], axis=0)


def local_stats(info, digits, student, teacher, pair, copies):
    tokens, unit = pair.shape[0] // 2, pair.shape[1]
    first = lambda i, info: (0, 0)
    return pl.pallas_call(
        stats_kernel,
        grid_spec=pltpu.PrefetchScalarGridSpec(
            num_scalar_prefetch=1,
            grid=(1,),
            in_specs=[
                pl.BlockSpec(digits.shape, first),
                pl.BlockSpec(student.shape, lambda i, info: (0, 0, 0)),
                pl.BlockSpec((tokens, unit), first),
                pl.BlockSpec((tokens, unit), lambda i, info: (1, 0)),
            ],
            out_specs=pl.BlockSpec((copies, stat_rows, 2 * tokens), lambda i, info: (0, 0, 0)),
        ),
        out_shape=jax.ShapeDtypeStruct((copies, stat_rows, 2 * tokens), jnp.float32),
        compiler_params=pltpu.CompilerParams(vmem_limit_bytes=32 * 2**20),
    )(info, digits, student, teacher, pair)


def teacher_regroup_kernel(head_ref, out_ref):
    unit = out_ref.shape[2]
    for j in range(out_ref.shape[0]):
        out_ref[j] = head_ref[:, j * unit : (j + 1) * unit]


def teacher_regroup(head, unit):
    depth, width = head.shape
    units = width // unit
    block = units // 2
    return pl.pallas_call(
        teacher_regroup_kernel,
        grid=(units // block,),
        in_specs=[pl.BlockSpec((depth, block * unit), lambda j: (0, j))],
        out_specs=pl.BlockSpec((block, depth, unit), lambda j: (j, 0, 0)),
        out_shape=jax.ShapeDtypeStruct((units, depth, unit), head.dtype),
        compiler_params=pltpu.CompilerParams(vmem_limit_bytes=big_vmem),
    )(head)


def teacher_kernel(own_ref, other_ref, cols_ref, out_ref):
    unit = out_ref.shape[2]
    count = own_ref.shape[0]
    for j in range(0, out_ref.shape[0], 2):
        cols = jnp.concatenate([cols_ref[j], cols_ref[j + 1]], axis=1)
        for start, rows_ref in ((0, own_ref), (count, other_ref)):
            part = jnp.dot(rows_ref[...], cols, preferred_element_type=jnp.float32)
            out_ref[j, start : start + count] = part[:, :unit]
            out_ref[j + 1, start : start + count] = part[:, unit:]


def teacher_partial(own, other, cols):
    units, depth, unit = cols.shape
    count = own.shape[0]
    block = units // 2
    return pl.pallas_call(
        teacher_kernel,
        grid=(units // block,),
        in_specs=[
            pl.BlockSpec((count, depth), lambda j: (0, 0)),
            pl.BlockSpec((count, depth), lambda j: (0, 0)),
            pl.BlockSpec((block, depth, unit), lambda j: (j, 0, 0)),
        ],
        out_specs=pl.BlockSpec((block, 2 * count, unit), lambda j: (j, 0, 0)),
        out_shape=jax.ShapeDtypeStruct((units, 2 * count, unit), jnp.float32),
        compiler_params=pltpu.CompilerParams(vmem_limit_bytes=big_vmem),
    )(own, other, cols)


def regroup_kernel(odd_ref, low_ref, high_ref, out_ref):
    unit = out_ref.shape[4]
    odd = odd_ref[0]
    for half, head_ref in enumerate((low_ref, high_ref)):
        for j in range(out_ref.shape[0]):
            row = 1 - odd if half != j % 2 else odd
            out_ref[j, row, 0] = head_ref[:, j * unit : (j + 1) * unit]


def regroup(odd, head, units, unit):
    rows, width = head.shape
    return pl.pallas_call(
        regroup_kernel,
        grid_spec=pltpu.PrefetchScalarGridSpec(
            num_scalar_prefetch=1,
            grid=(2,),
            in_specs=[
                pl.BlockSpec((rows, width // 4), lambda core, odd: (0, core)),
                pl.BlockSpec((rows, width // 4), lambda core, odd: (0, 2 + core)),
            ],
            out_specs=pl.BlockSpec(
                (units, 2, 1, rows, unit), lambda core, odd: (0, 0, core, 0, 0)
            ),
        ),
        out_shape=jax.ShapeDtypeStruct((units, 2, 2, rows, unit), head.dtype),
        compiler_params=pltpu.CompilerParams(vmem_limit_bytes=32 * 2**20),
    )(odd, head, head)


def student_kernel(core_ref, rows_ref, own_mine, own_pair, far_mine, far_pair, out_ref, turned_ref):
    core = core_ref[0]
    slices, _, depth = rows_ref.shape
    part, unit = own_mine.shape[2], own_mine.shape[3]
    own_rows, far_rows = [], []
    for k in range(slices):
        for start in range(0, depth, 2 * part):
            near = pl.multiple_of(start + core * part, part)
            away = pl.multiple_of(start + part - core * part, part)
            own_rows.append(rows_ref[k, :, pl.ds(near, part)])
            far_rows.append(rows_ref[k, :, pl.ds(away, part)])
    own_rows = jnp.concatenate(own_rows, axis=1)
    far_rows = jnp.concatenate(far_rows, axis=1)

    @pl.when(pl.program_id(0) == 0)
    def _():
        for h, cols_ref in enumerate((own_mine, own_pair)):
            turned_ref[0, h] = cols_ref[:, 0].reshape(-1, unit).T

    @pl.when(pl.program_id(0) == 1)
    def _():
        for h, cols_ref in enumerate((far_mine, far_pair)):
            turned_ref[0, h] = cols_ref[:, 0].reshape(-1, unit).T

    for h, (own_ref, far_ref) in enumerate(((own_mine, far_mine), (own_pair, far_pair))):
        out_ref[h] = jnp.dot(
            own_rows, own_ref[:, 0].reshape(-1, unit), preferred_element_type=jnp.float32
        ) + jnp.dot(far_rows, far_ref[:, 0].reshape(-1, unit), preferred_element_type=jnp.float32)


def student_full(core, rows, own, far):
    slices, tokens, depth = rows.shape
    groups, _, part, unit = own.shape
    block = tokens // 2
    cols = (groups, 1, part, unit)
    mine = pl.BlockSpec(cols, lambda i, core: (0, core[0], 0, 0))
    pair = pl.BlockSpec(cols, lambda i, core: (0, 1 - core[0], 0, 0))
    return pl.pallas_call(
        student_kernel,
        grid_spec=pltpu.PrefetchScalarGridSpec(
            num_scalar_prefetch=1,
            grid=(tokens // block,),
            in_specs=[
                pl.BlockSpec((slices, block, depth), lambda i, core: (0, i, 0)),
                mine,
                pair,
                mine,
                pair,
            ],
            out_specs=[
                pl.BlockSpec((2, block, unit), lambda i, core: (0, i, 0)),
                pl.BlockSpec((1, 2, unit, groups * part), lambda i, core: (i, 0, 0, 0)),
            ],
        ),
        out_shape=[
            jax.ShapeDtypeStruct((2, tokens, unit), jnp.float32),
            jax.ShapeDtypeStruct((2, 2, unit, groups * part), own.dtype),
        ],
        compiler_params=pltpu.CompilerParams(vmem_limit_bytes=48 * 2**20),
    )(core, rows, own, own, far, far)


def grad_kernel(
    info_ref, stats_ref, digits_ref, student_ref, own_ref, pair_ref,
    turned_ref, out_ref, loss_ref, grad_ref,
):
    core = info_ref[0]
    unit = turned_ref.shape[2]
    tokens = out_ref.shape[0]
    part = lanes
    block = turned_ref.shape[3] // part

    @pl.when(pl.program_id(0) == 0)
    def _():
        tops, sums, cross, picked = merged(stats_ref[...])
        norms = tops + jnp.log(sums)
        student_norm, teacher_norm = norms[:, :tokens], norms[:, tokens:]
        gap = cross / sums[:, :tokens]
        loss = gap - student_norm + teacher_norm + ce_weight * (student_norm - picked)
        loss_ref[...] = jnp.broadcast_to(loss, loss_ref.shape)
        row = lax.broadcasted_iota(jnp.int32, (lanes, tokens), 0)
        table = jnp.where(row == 0, student_norm, jnp.where(row == 1, gap, 0.0)).T
        for h, teacher_ref in enumerate((own_ref, pair_ref)):
            student = student_ref[h]
            prob = jnp.exp(student - table[:, 0:1])
            found = hits(info_ref, h, digits_ref, (tokens, unit)).astype(jnp.float32)
            grad = prob * ((student - teacher_ref[...]) - table[:, 1:2])
            grad_ref[h] = (grad + ce_weight * (prob - found)).astype(grad_ref.dtype)

    for near, which in ((core, 0), (1 - core, 1)):
        total = jnp.dot(
            grad_ref[0], turned_ref[which, 0], preferred_element_type=jnp.float32
        ) + jnp.dot(grad_ref[1], turned_ref[which, 1], preferred_element_type=jnp.float32)
        total = total.astype(out_ref.dtype)
        for m in range(block):
            start = pl.multiple_of((2 * m + near) * part, part)
            out_ref[:, pl.ds(start, part)] = total[:, m * part : (m + 1) * part]


def grad_partial(info, stats, digits, student, teacher_own, teacher_pair, turned):
    _, tokens, unit = student.shape
    width = turned.shape[3]
    block = width // 4
    whole = [
        pl.BlockSpec(shape, lambda i, info, n=len(shape): (0,) * n)
        for shape in (
            stats.shape, digits.shape, student.shape, (tokens, unit)
        )
    ]
    whole.append(pl.BlockSpec((tokens, unit), lambda i, info: (1, 0)))
    return pl.pallas_call(
        grad_kernel,
        grid_spec=pltpu.PrefetchScalarGridSpec(
            num_scalar_prefetch=1,
            grid=(width // block,),
            in_specs=whole + [pl.BlockSpec((2, 2, unit, block), lambda i, info: (0, 0, 0, i))],
            out_specs=[
                pl.BlockSpec((tokens, 2 * block), lambda i, info: (0, i)),
                pl.BlockSpec((stat_rows, tokens), lambda i, info: (0, 0)),
            ],
            scratch_shapes=[pltpu.VMEM((2, tokens, unit), jnp.bfloat16)],
        ),
        out_shape=[
            jax.ShapeDtypeStruct((tokens, 2 * width), jnp.bfloat16),
            jax.ShapeDtypeStruct((stat_rows, tokens), jnp.float32),
        ],
        compiler_params=pltpu.CompilerParams(vmem_limit_bytes=40 * 2**20),
    )(info, stats, digits, student, teacher_own, teacher_pair, turned)


def sum_kernel(parts_ref, out_ref):
    share = out_ref.shape[2]
    for k in range(out_ref.shape[0]):
        part = parts_ref[:, :, k * share : (k + 1) * share].astype(jnp.float32)
        out_ref[k] = jnp.sum(part, axis=0).astype(out_ref.dtype)


def plane_sums(parts, count):
    _, rows, width = parts.shape
    whole = pl.BlockSpec(memory_space=pltpu.VMEM)
    return pl.pallas_call(
        sum_kernel,
        in_specs=[whole],
        out_specs=whole,
        out_shape=jax.ShapeDtypeStruct((count, rows, width // count), parts.dtype),
        compiler_params=pltpu.CompilerParams(vmem_limit_bytes=16 * 2**20),
    )(parts)


def copies_kernel(parts_ref, out_ref):
    total = jnp.sum(parts_ref[...].astype(jnp.float32), axis=0).astype(out_ref.dtype)
    out_ref[...] = jnp.broadcast_to(total, out_ref.shape)


def summed_copies(parts):
    whole = pl.BlockSpec(memory_space=pltpu.VMEM)
    return pl.pallas_call(
        copies_kernel,
        in_specs=[whole],
        out_specs=whole,
        out_shape=jax.ShapeDtypeStruct(parts.shape, parts.dtype),
        compiler_params=pltpu.CompilerParams(vmem_limit_bytes=16 * 2**20),
    )(parts)


def local(student_hidden, teacher_hidden, student_head, teacher_head, sampled_ids):
    core = lax.axis_index("c")
    core_id = core.reshape(1).astype(jnp.int32)
    plane = lax.axis_index("z")
    tok, width = student_hidden.shape
    xy_count = lax.axis_size(XY)
    z_count = lax.axis_size("z")
    row_part = student_head.shape[0]
    unit = teacher_head.shape[1] // z_count
    depth = teacher_head.shape[0]
    share = width // z_count

    pay = jnp.concatenate(
        [
            lax.dynamic_slice_in_dim(teacher_hidden, plane * depth, depth, 1),
            lax.dynamic_slice_in_dim(student_hidden, plane * share, share, 1),
        ],
        axis=1,
    )
    teacher_head, student_head, sampled_ids, pay = lax.optimization_barrier(
        (teacher_head, student_head, sampled_ids, pay)
    )
    gathered = spread(pay, XY).reshape(-1, depth + share)
    tokens = gathered.shape[0]

    teacher_parts = teacher_regroup(teacher_head, unit)
    odd_plane = lax.rem(plane, 2)
    parts = regroup(odd_plane.reshape(1).astype(jnp.int32), student_head, z_count, unit)
    parts = parts.reshape(xy_count, 2, row_part, unit)
    digits = jnp.stack(
        [sampled_ids // (digit * digit), sampled_ids // digit % digit, sampled_ids % digit], axis=1
    ).astype(jnp.bfloat16)
    digits = jnp.pad(digits, ((0, 0), (0, lanes - 3)))
    teacher_other = swap_cores(gathered[:, :depth])
    share_rows = gathered[:, depth:]
    teacher_parts, gathered, teacher_other, share_rows, parts, digits = lax.optimization_barrier(
        (teacher_parts, gathered, teacher_other, share_rows, parts, digits)
    )

    student_rows = lax.all_gather(share_rows, "z", axis=0, tiled=False)
    teacher_cols = lax.all_to_all(
        teacher_parts, XY, 0, 0, axis_index_groups=near_groups, tiled=True
    )
    teacher_part = teacher_partial(gathered, teacher_other, teacher_cols)

    parts, student_rows, teacher_part = lax.optimization_barrier(
        (parts, student_rows, teacher_part)
    )
    teacher_sum = lax.psum_scatter(
        teacher_part.reshape(-1, unit), "z", scatter_dimension=0, tiled=True
    )
    own_cols = exchange(parts, XY)
    far_cols = swap_cores(own_cols)
    student_logits, turned = student_full(core_id, student_rows, own_cols, far_cols)
    digits, place, turned = lax.optimization_barrier((digits, lax.axis_index(XY), turned))
    id_digits = spread(digits, XY).reshape(tokens, lanes)
    teacher_sum, id_digits = lax.optimization_barrier((teacher_sum, id_digits))
    teacher_pair = swap_cores(teacher_sum)

    row = lax.rem(place, 4)
    xyh = place // 2
    near = lax.rem(row // 2 + row, 2)
    cores = jnp.stack([core, 1 - core]).astype(jnp.int32)
    owner = (plane * 2 + lax.rem(near + plane, 2)) * 2 + cores
    info = jnp.concatenate([core_id, (owner * z_count + xyh) * unit])

    stats = local_stats(info, id_digits, student_logits, teacher_sum, teacher_pair, xy_count)
    stats = spread(merge(exchange(stats, XY)), "z")
    grad_part, losses = grad_partial(
        info, stats, id_digits, student_logits, teacher_sum, teacher_pair, turned
    )
    token_loss = lax.dynamic_slice_in_dim(losses[0], lax.axis_index(XY) * tok, tok, 0)
    grad_part = grad_part.reshape(xy_count, tok, width)
    plane_part = plane_sums(exchange(grad_part, XY), z_count)
    final = exchange(summed_copies(exchange(plane_part, "z")), "z")
    grad_hidden = final.transpose(1, 0, 2).reshape(tok, width)
    return (grad_hidden, token_loss)


def solution(mesh):
    fine = Mesh(mesh.devices.reshape(16, 2, 8), ("xy", "c", "z"))
    in_specs = (P(DP, None), P(DP, None), P(DP, "z"), P("z", DP), P(DP))
    out_specs = (P(DP, None), P(DP))
    return jax.shard_map(local, mesh=fine, in_specs=in_specs, out_specs=out_specs, check_vma=False)
```
